32 devices in a mesh: pipe: 4 (over y, x), rows: 8 (over z, core).
Axes of the slice: x: 2, y: 2, z: 4, core: 2. Of those that a mesh axis runs over, the one named last changes fastest.
Arguments:
- features: bfloat16 [128, 65536], P('pipe', 'rows'), may hold values from 0 to 16
- weights: bfloat16 [8, 1024, 64, 256], P('pipe', 'rows'), may hold values from -0.5 to 0.5
- bias: bfloat16 [8, 65536], P('pipe', 'rows'), may hold values from -2 to 2
- layout: int32 [8, 4096], P('pipe'), may hold values from 0 to 1023, as said below
Outputs:
- activations: bfloat16 [128, 65536], P('pipe', 'rows')
The draws below stay inside these ranges and needn't reach their ends.
Inputs may be any that keep to these rules, and one draw needn't show every extreme that they name: `layout`: for every layer and every index of rows, the 512 slots of that index's 128 output blocks read blocks held by exactly 8 distinct indices of rows (index = block // 128), exactly 64 slots from each of them.
All inputs are finite; a program needn't handle non-finite values.
Results may differ from the reference program's by a relative error of at most 0.013.
Values may be sent and summed in bfloat16 or wider, within the bound.
No kernel may reach another device: no remote copies, remote signals or barrier semaphores. Data moves between devices by JAX's collectives and lax.ppermute only.
A program may use at most 192 MiB of HBM per device.

```python
import jax
import jax.numpy as jnp
from jax import lax

NEURONS = 65536
BLOCK = 64
K = 4
LAYERS = 8
BATCH = 128
NB = 1024
BD = 128
SLOTS = 512
GROUPS = 8
N_ROWS = 8


def draw_layout(key, part):

    def one_group(inner_key):
        first_key, second_key, third_key = jax.random.split(inner_key, 3)
        owners = jax.random.permutation(first_key, N_ROWS)[:GROUPS]
        ordering = jax.random.permutation(second_key, SLOTS)
        sources = owners[ordering % GROUPS]
        locals_drawn = jax.random.randint(third_key, (SLOTS,), 0, BD)
        return (sources * BD + locals_drawn).astype(jnp.int32)
    all_keys = jax.random.split(jax.random.fold_in(key, 7), LAYERS * N_ROWS)
    return jax.vmap(one_group)(all_keys).reshape(LAYERS, NB * K)


def shard_levels(rng, dims, pieces, smallest, top_value):
    loudness, own = 1.0, jax.random.fold_in(rng, 6)
    for position, blocks in pieces:
        heights = jnp.exp(jax.random.uniform(jax.random.fold_in(own, position), (blocks,), jnp.float32, smallest / len(pieces), top_value / len(pieces)))
        loudness = loudness * jnp.repeat(heights, dims[position] // blocks).reshape([-1 if axis == position else 1 for axis in range(len(dims))])
    return loudness


def normal_values(key, dims, width, bound, shards=(), held_as=jnp.bfloat16):
    array = jax.random.normal(key, dims, jnp.float32) * width
    if len(shards) > 0:
        array = shard_levels(key, dims, shards, -0.22, 0.18) * array
    return jnp.clip(array, min=-bound, max=bound).astype(held_as)


def setup_inputs(seed: int = 0) -> dict:
    splits = jax.random.split(jax.random.key(seed), 5)
    return {
        "features": jnp.clip(16.0 * jax.random.uniform(splits[0], (BATCH, NEURONS), jnp.float32) ** shard_levels(splits[0], (BATCH, NEURONS), ((0, 4), (1, 8)), -0.2, 0.2), 0.0, 16.0).astype(jnp.bfloat16),
        "weights": normal_values(splits[1], (LAYERS, NB, BLOCK, K * BLOCK), (K * BLOCK // 2) ** -0.5, 0.5, ((0, 4), (1, 8))),
        "bias": jnp.clip(jax.random.uniform(splits[2], (LAYERS, NEURONS), jnp.float32, -2.0, 2.0) * shard_levels(splits[2], (LAYERS, NEURONS), ((0, 4), (1, 8)), -0.4, 0.0), -2.0, 2.0).astype(jnp.bfloat16),
        "layout": draw_layout(jax.random.fold_in(splits[4], 71), 0),
    }


clamp_top = 32.0
span_blocks = 16


def reference(features, weights, bias, layout):
    current = features.reshape(BATCH, NB, BLOCK)
    for layer_idx in range(LAYERS):
        index_parts = layout[layer_idx].reshape(NB // span_blocks, span_blocks * K)
        reordered = jnp.transpose(weights[layer_idx].reshape(NB, BLOCK, K, BLOCK), (0, 2, 1, 3))
        weight_parts = reordered.reshape(NB // span_blocks, span_blocks * K, BLOCK, BLOCK)

        def one_span(pair):
            indices, weight_span = pair
            inputs = jnp.take(current, indices, axis=1).astype(jnp.float32)
            products = jnp.einsum('rsf,sfg->rsg', inputs, weight_span.astype(jnp.float32))
            return products.reshape(BATCH, span_blocks, K, BLOCK).sum(axis=2)

        spans = lax.map(one_span, (index_parts, weight_parts))
        summed = jnp.transpose(spans, (1, 0, 2, 3)).reshape(BATCH, NB * BLOCK)
        summed = summed + bias[layer_idx].astype(jnp.float32)[None, :]
        current = jnp.clip(jax.nn.relu(summed), 0.0, clamp_top).astype(jnp.bfloat16).reshape(BATCH, NB, BLOCK)
    return current.reshape(BATCH, NEURONS)
```

```python
import functools

import jax
import jax.numpy as jnp
import numpy as np
from jax import lax
from jax.experimental import pallas as pl
from jax.experimental.pallas import tpu as pltpu
from jax.sharding import PartitionSpec as P

BLOCK = 64
K = 4
LANES = 128
CORES = 2
WEIGHT_PARTS = 4

clamp_top = 32.0


def layer_kernel(act_plan, weight_plan, unroll, codes, place, *refs):
    n_acts = 1 + max(p[0] for p in act_plan)
    n_weights = 1 + max(p[0] for p in weight_plan)
    acts, weights = refs[:n_acts], refs[n_acts : n_acts + n_weights]
    bias, out, held, wheld, masks, act_sem, w_sem = refs[n_acts + n_weights :]
    rows = out.shape[0]
    blocks = wheld.shape[0]
    pairs = held.shape[2] // LANES

    def start(copy, want):
        if want is None:
            copy.start()
        else:
            pl.when(place[want[0]] == want[1])(copy.start)

    def act_copy(operand, slot, slots):
        src = acts[operand] if slots == 1 else acts[operand].at[:]
        dst = held.at[slot] if slots == 1 else held.at[pl.ds(slot, slots)]
        return pltpu.make_async_copy(src, dst, act_sem.at[slot])

    def weight_copy(operand, first, count, index):
        src = weights[operand] if index is None else weights[operand].at[index]
        part = wheld.at[pl.ds(first, count)]
        return pltpu.make_async_copy(src, part, w_sem.at[first])

    for operand, slot, slots, want in act_plan:
        start(act_copy(operand, slot, slots), want)
    for operand, first, count, index, want in weight_plan:
        start(weight_copy(operand, first, count, index), want)

    low = lax.broadcasted_iota(jnp.int32, (rows, LANES), 1) < BLOCK
    masks[0] = jnp.where(low, 1.0, 0.0).astype(jnp.bfloat16)
    masks[1] = jnp.where(low, 0.0, 1.0).astype(jnp.bfloat16)

    waited = set()
    for operand, slot, slots, _ in act_plan:
        if slot not in waited:
            waited.add(slot)
            act_copy(operand, slot, slots).wait()

    def products(block):
        parts = []
        for k in range(K):
            code = codes[block * K + k]
            pair = lax.rem(code // 2, pairs)
            columns = pl.ds(pl.multiple_of(pair * LANES, LANES), LANES)
            parts.append(held[code // (2 * pairs), :, columns] * masks[lax.rem(code, 2)])
        left = jnp.concatenate(
            [
                jnp.concatenate([parts[0], parts[2]], axis=1),
                jnp.concatenate([parts[1], parts[3]], axis=1),
            ],
            axis=0,
        )
        w = wheld[block]
        first, second = w[:, :LANES], w[:, LANES:]
        right = jnp.concatenate([first, first, second, second], axis=0)
        return jnp.dot(left, right, preferred_element_type=jnp.float32)

    def two_blocks(q, _):
        a, b = products(2 * q), products(2 * q + 1)
        even = a[:rows] + pltpu.roll(a[rows:], BLOCK, 1)
        odd = b[rows:] + pltpu.roll(b[:rows], BLOCK, 1)
        columns = pl.ds(pl.multiple_of(q * LANES, LANES), LANES)
        total = jnp.where(low, even, odd) + bias[:, columns].astype(jnp.float32)
        out[:, columns] = jnp.clip(total, 0.0, clamp_top).astype(jnp.bfloat16)
        return 0

    parts = sorted({(first, count) for _, first, count, _, _ in weight_plan})
    for first, count in parts:
        entry = next(p for p in weight_plan if p[1] == first)
        weight_copy(*entry[:4]).wait()
        steps = count // 2
        lax.fori_loop(first // 2, first // 2 + steps, two_blocks, 0, unroll=min(unroll, steps))


def apply_layer(codes, place, acts, act_plan, weights, weight_plan, bias):
    slots = sum(
        count for slot, count in {(slot, count) for _, slot, count, _ in act_plan}
    )
    rows, neurons = acts[0].shape[-2:]
    blocks = neurons // BLOCK
    held = (slots, rows, neurons)
    wheld = (blocks, BLOCK, K * BLOCK)
    smem = pl.BlockSpec(memory_space=pltpu.SMEM)
    anywhere = pl.BlockSpec(memory_space=pl.ANY)
    vmem = pl.BlockSpec(memory_space=pltpu.VMEM)
    kernel = functools.partial(layer_kernel, act_plan, weight_plan, 8)
    return pl.pallas_call(
        kernel,
        out_shape=jax.ShapeDtypeStruct((rows, neurons), jnp.bfloat16),
        in_specs=[smem, smem] + [anywhere] * (len(acts) + len(weights)) + [vmem],
        out_specs=vmem,
        scratch_shapes=[
            pltpu.VMEM(held, jnp.bfloat16),
            pltpu.VMEM(wheld, jnp.bfloat16),
            pltpu.VMEM((2, rows, LANES), jnp.bfloat16),
            pltpu.SemaphoreType.DMA((slots,)),
            pltpu.SemaphoreType.DMA((blocks,)),
        ],
        compiler_params=pltpu.CompilerParams(vmem_limit_bytes=32 * 2**20),
    )(codes, place, *acts, *weights, bias)


def along_line(x, pairs):
    moves = [(a * CORES + c, b * CORES + c) for a, b in pairs for c in range(CORES)]
    return lax.ppermute(x, "rows", moves)


def to_other_core(x, chips):
    moves = [(z * CORES + c, z * CORES + 1 - c) for z in chips for c in range(CORES)]
    return lax.ppermute(x, "rows", moves)


def gather_line(x):
    ends, middle, every = (0, 3), (1, 2), (0, 1, 2, 3)
    near = along_line(x, [(0, 1), (1, 0), (2, 3), (3, 2)])
    inner = along_line(x, [(1, 2), (2, 1)])
    far = along_line(near, [(1, 2), (2, 1)])
    outer = along_line(inner, [(2, 3), (1, 0)])
    last = along_line(far, [(2, 3), (1, 0)])
    own_side = [x, near, inner, far, outer, last]
    other_side = [
        to_other_core(buf, chips)
        for buf, chips in zip(own_side, (every, every, middle, middle, ends, ends))
    ]
    return own_side + other_side


def line_plan():
    plan = []
    for side in range(CORES):
        for buf, (slot, want) in enumerate(
            [(0, None), (1, None), (2, (0, 1)), (3, (0, 1)), (2, (0, 0)), (3, (0, 0))]
        ):
            plan.append((side * 6 + buf, side * 4 + slot, 1, want))
    return plan


def line_slots(row_devs):
    table = np.zeros((row_devs, row_devs), np.int32)
    chips = row_devs // CORES
    for me in range(row_devs):
        for owner in range(row_devs):
            z, c = divmod(me, CORES)
            oz, oc = divmod(owner, CORES)
            far = [chip for chip in range(chips) if chip // 2 != z // 2]
            if oz // 2 == z // 2:
                slot = 0 if oz == z else 1
            else:
                nearest = min(far, key=lambda chip: abs(chip - z))
                slot = 2 if oz == nearest else 3
            table[me, owner] = (c != oc) * chips + slot
    return table


def on_device(features, weights, bias, layout):
    row_devs = lax.axis_size("rows")
    my_row = lax.axis_index("rows")
    neurons = features.shape[1]
    blocks = neurons // BLOCK
    slot_count = blocks * K
    pairs = neurons // LANES
    is_line = row_devs == 4 * CORES

    mine = lax.dynamic_slice_in_dim(layout, my_row * slot_count, slot_count, axis=1)
    owners, local = mine // blocks, mine % blocks
    table = line_slots(row_devs) if is_line else np.tile(np.arange(row_devs, dtype=np.int32), (row_devs, 1))
    my_slots = lax.dynamic_index_in_dim(jnp.asarray(table), my_row, 0, keepdims=False)
    hit = owners[:, :, None] == jnp.arange(row_devs)[None, None, :]
    slots = jnp.sum(jnp.where(hit, my_slots[None, None, :], 0), axis=2)
    codes = (slots * pairs + local // 2) * 2 + local % 2

    all_codes = lax.all_gather(codes, "pipe", axis=0, tiled=True)
    all_bias = lax.all_gather(bias, "pipe", axis=0, tiled=True)
    all_weights = lax.all_gather(weights, "pipe", axis=0, tiled=True)
    z = my_row // CORES
    is_middle = (z > 0) & (z < row_devs // CORES - 1)
    place = jnp.stack([is_middle.astype(jnp.int32)])

    current = features
    parts = min(WEIGHT_PARTS, blocks // 2)
    each = blocks // parts
    for layer in range(all_weights.shape[0]):
        if is_line:
            acts, act_plan = gather_line(current), line_plan()
        else:
            acts = [lax.all_gather(current, "rows", axis=0, tiled=False)]
            act_plan = [(0, 0, row_devs, None)]
        weight_plan = [
            (0, i * each, each, (layer, pl.ds(i * each, each)), None) for i in range(parts)
        ]
        current = apply_layer(
            all_codes[layer], place, acts, act_plan, [all_weights], weight_plan, all_bias[layer][None]
        )
    return current


def solution(mesh):
    in_specs = (
        P("pipe", "rows"),
        P("pipe", "rows", None, None),
        P("pipe", "rows"),
        P("pipe", None),
    )
    out_specs = P("pipe", "rows")
    return jax.shard_map(
        on_device, mesh=mesh, in_specs=in_specs, out_specs=out_specs, check_vma=False
    )
```

```python
import functools
import random

import jax
import jax.numpy as jnp
import numpy as np
from jax import lax
from jax.experimental import pallas as pl
from jax.experimental.pallas import tpu as pltpu
from jax.sharding import PartitionSpec as P

BLOCK = 64
K = 4
LANES = 128
CORES = 2
WEIGHT_PARTS = 4
STREAM_SEED = 486
LAYER_VMEM = 10 * 2**20
SMALL_VMEM = 2 * 2**20

clamp_top = 32.0


def bits_for(count):
    return (count - 1).bit_length()


def start_if(copy, place, want):
    if want is None:
        copy.start()
    else:
        pl.when(place[want[0]] == want[1])(copy.start)


def layer_kernel(act_plan, unroll, codes, place, *refs):
    n_acts = 1 + max(p[0] for p in act_plan)
    acts = refs[:n_acts]
    weights, bias, out, held, masks, act_sem = refs[n_acts:]
    rows = out.shape[0]
    blocks = weights.shape[0]
    pair_bits = bits_for(held.shape[2] // LANES)

    def act_copy(operand, slot, slots):
        src = acts[operand] if slots == 1 else acts[operand].at[:]
        dst = held.at[slot] if slots == 1 else held.at[pl.ds(slot, slots)]
        return pltpu.make_async_copy(src, dst, act_sem.at[slot])

    for operand, slot, slots, want in act_plan:
        start_if(act_copy(operand, slot, slots), place, want)

    low = lax.broadcasted_iota(jnp.int32, (rows, LANES), 1) < BLOCK
    masks[0] = jnp.where(low, 1.0, 0.0).astype(jnp.bfloat16)
    masks[1] = jnp.where(low, 0.0, 1.0).astype(jnp.bfloat16)

    waited = set()
    for operand, slot, slots, _ in act_plan:
        if slot not in waited:
            waited.add(slot)
            act_copy(operand, slot, slots).wait()

    def products(block):
        parts = []
        for k in range(K):
            code = codes[block * K + k]
            pair = (code >> 1) & (2**pair_bits - 1)
            columns = pl.ds(pl.multiple_of(pair * LANES, LANES), LANES)
            parts.append(held[code >> (1 + pair_bits), :, columns] * masks[code & 1])
        left = jnp.concatenate(
            [
                jnp.concatenate([parts[0], parts[2]], axis=1),
                jnp.concatenate([parts[1], parts[3]], axis=1),
            ],
            axis=0,
        )
        w = weights[block]
        first, second = w[:, :LANES], w[:, LANES:]
        right = jnp.concatenate([first, first, second, second], axis=0)
        return jnp.dot(left, right, preferred_element_type=jnp.float32)

    def two_blocks(q, _):
        a, b = products(2 * q), products(2 * q + 1)
        even = a[:rows] + pltpu.roll(a[rows:], BLOCK, 1)
        odd = b[rows:] + pltpu.roll(b[:rows], BLOCK, 1)
        columns = pl.ds(pl.multiple_of(q * LANES, LANES), LANES)
        total = jnp.where(low, even, odd) + bias[:, columns].astype(jnp.float32)
        out[:, columns] = jnp.clip(total, 0.0, clamp_top).astype(jnp.bfloat16)
        return 0

    lax.fori_loop(0, blocks // 2, two_blocks, 0, unroll=min(unroll, blocks // 2))


def gather_weights_kernel(plan, place, *refs):
    sources, out, sem = refs[:-2], refs[-2], refs[-1]

    def copy(operand, first, count, index):
        source = sources[operand] if index is None else sources[operand].at[index]
        return pltpu.make_async_copy(source, out.at[pl.ds(first, count)], sem.at[first])

    for operand, first, count, index, want in plan:
        start_if(copy(operand, first, count, index), place, want)
    for first, (operand, count, index) in {p[1]: (p[0], p[2], p[3]) for p in plan}.items():
        copy(operand, first, count, index).wait()


def gather_weights(place, weights, plan, shape):
    smem = pl.BlockSpec(memory_space=pltpu.SMEM)
    return pl.pallas_call(
        functools.partial(gather_weights_kernel, plan),
        out_shape=pltpu.VMEM(shape, jnp.bfloat16),
        in_specs=[smem] + [pl.BlockSpec(memory_space=pl.ANY)] * len(weights),
        out_specs=pl.BlockSpec(memory_space=pltpu.VMEM),
        scratch_shapes=[pltpu.SemaphoreType.DMA((shape[0],))],
        compiler_params=pltpu.CompilerParams(vmem_limit_bytes=SMALL_VMEM),
    )(place, *weights)


def apply_layer(codes, place, acts, act_plan, weights, bias):
    slots = sum(
        count for slot, count in {(slot, count) for _, slot, count, _ in act_plan}
    )
    rows, neurons = acts[0].shape[-2:]
    held = (slots, rows, neurons)
    smem = pl.BlockSpec(memory_space=pltpu.SMEM)
    anywhere = pl.BlockSpec(memory_space=pl.ANY)
    vmem = pl.BlockSpec(memory_space=pltpu.VMEM)
    kernel = functools.partial(layer_kernel, act_plan, 16)
    return pl.pallas_call(
        kernel,
        out_shape=jax.ShapeDtypeStruct((rows, neurons), jnp.bfloat16),
        in_specs=[smem, smem] + [anywhere] * len(acts) + [vmem, vmem],
        out_specs=vmem,
        scratch_shapes=[
            pltpu.VMEM(held, jnp.bfloat16),
            pltpu.VMEM((2, rows, LANES), jnp.bfloat16),
            pltpu.SemaphoreType.DMA((slots,)),
        ],
        compiler_params=pltpu.CompilerParams(vmem_limit_bytes=LAYER_VMEM),
    )(codes, place, *acts, weights, bias)


def along_line(x, pairs):
    moves = [(a * CORES + c, b * CORES + c) for a, b in pairs for c in range(CORES)]
    return lax.ppermute(x, "rows", moves)


def to_other_core(x):
    return lax.ppermute(x, "rows", [(i, i ^ 1) for i in range(lax.axis_size("rows"))])


def gather_line(x, pause):
    near = along_line(x, [(0, 1), (1, 0), (2, 3), (3, 2)])
    cross = along_line(x, [(1, 2), (2, 1), (0, 3), (3, 0)])
    x_swapped = to_other_core(x)
    near, cross = pause(x_swapped, [near, cross])
    far = along_line(near, [(1, 2), (2, 1)])
    outer = along_line(cross, [(2, 3), (1, 0)])
    near_swapped = to_other_core(near)
    far, outer = pause(near_swapped, [far, outer])
    rest = [cross, far, outer]
    return [x, near] + rest + [x_swapped, near_swapped] + [to_other_core(buf) for buf in rest]


def line_plan():
    plan = []
    for side in range(CORES):
        for buf, (slot, want) in enumerate([(0, None), (1, None), (2, None), (3, (0, 1)), (3, (0, 0))]):
            plan.append((side * 5 + buf, side * 4 + slot, 1, want))
    return plan


def line_slots(row_devs):
    table = np.zeros((row_devs, row_devs), np.int32)
    chips = row_devs // CORES
    for me in range(row_devs):
        for owner in range(row_devs):
            z, c = divmod(me, CORES)
            oz, oc = divmod(owner, CORES)
            if oz // 2 == z // 2:
                slot = 0 if oz == z else 1
            else:
                across = chips - 1 - z
                slot = 2 if oz == across else 3
            table[me, owner] = (c != oc) * chips + slot
    return table


def stream_order(seed, layers, parts, square):
    draw = random.Random(seed)
    each = layers // square
    links = [(u, u ^ 1) for u in range(square)] + [(u, u ^ 2) for u in range(square)]
    pieces = [(layer, q) for layer in range(layers) for q in range(parts)]
    have = {(p, piece): 0 for p in range(square) for piece in pieces if piece[0] // each == p}
    noise, direct, spread = draw.choice([0, 0.3, 1, 2]), draw.choice([0, 1, 2]), draw.choice([0, 0.5, 1, 2])
    slots = []
    while len(have) < square * len(pieces):
        now, sends = len(slots), []
        taken = set()
        order = links[:]
        draw.shuffle(order)
        if now == 0:
            sends = [(u, v, (u * each, 0 if u ^ v == 1 else 1)) for u, v in links]
            order = []
        for u, v in order:
            best = None
            for piece in pieces:
                if (v, piece) in have or (v, piece) in taken or have.get((u, piece), now + 1) > now:
                    continue
                w = v ^ 1 if u == v ^ 2 else v ^ 2
                holders = sum((p, piece) in have or (p, piece) in taken for p in range(square))
                also = have.get((w, piece), now + 1) <= now
                key = piece[0] * 4 + direct * also + spread * holders + noise * draw.random()
                if best is None or key < best[0]:
                    best = (key, piece)
            if best is not None:
                taken.add((v, best[1]))
                sends.append((u, v, best[1]))
        for u, v, piece in sends:
            have[v, piece] = now + 1
        slots.append(sends)
    ready = [max(have[p, (layer, q)] for p in range(square) for q in range(parts)) for layer in range(layers)]
    return slots, ready


def pick_kernel(choices, count, place, *refs):
    sources, outs, sems = refs[:-count - 1], refs[-count - 1 : -1], refs[-1]

    def copy_for(p):
        copies = []
        for n, per_device in enumerate(choices):
            operand, index = per_device[p]
            source = sources[operand] if index is None else sources[operand].at[index]
            copies.append(pltpu.make_async_copy(source, outs[n], sems.at[n]))
        for copy in copies:
            copy.start()
        for copy in copies:
            copy.wait()

    for p in range(len(choices[0])):
        pl.when(place[1] == p)(functools.partial(copy_for, p))


def pick(place, operands, choices, shape):
    smem = pl.BlockSpec(memory_space=pltpu.SMEM)
    return pl.pallas_call(
        functools.partial(pick_kernel, choices, len(choices)),
        out_shape=[pltpu.VMEM(shape, jnp.bfloat16)] * len(choices),
        in_specs=[smem] + [pl.BlockSpec(memory_space=pl.ANY)] * len(operands),
        out_specs=[pl.BlockSpec(memory_space=pltpu.VMEM)] * len(choices),
        scratch_shapes=[pltpu.SemaphoreType.DMA((len(choices),))],
        compiler_params=pltpu.CompilerParams(vmem_limit_bytes=SMALL_VMEM),
    )(place, *operands)


class WeightStream:
    def __init__(self, weights, place, square, parts):
        self.weights, self.place = weights, place
        self.sections, self.parts = weights.shape[0], parts
        self.each = weights.shape[1] // parts
        self.slots, self.ready = stream_order(STREAM_SEED, square * self.sections, parts, square)
        self.square = square
        self.arrays = {}
        self.where = {}
        self.flying = []
        self.started = 0
        self.gathered = {}

    def source(self, p, piece):
        if piece is None:
            piece = (p * self.sections, 0)
        if (p, piece) in self.where:
            return self.where[p, piece], None
        return "own", (piece[0] % self.sections, pl.ds(piece[1] * self.each, self.each))

    def array(self, name):
        return self.weights if name == "own" else self.arrays[name]

    def advance(self, after=(), through=(), layer=None):
        sends = self.slots[self.started] if self.started < len(self.slots) else []
        sides = {}
        for u, v, piece in sends:
            sides.setdefault(u ^ v, {})[u] = piece
        chosen = {side: [self.source(p, by.get(p)) for p in range(self.square)] for side, by in sorted(sides.items())}
        names = sorted({name for items in chosen.values() for name, _ in items}, key=str)
        keys = self.flying + [n for n in names if n != "own" and n not in self.flying]
        _, held = lax.optimization_barrier((list(after), [self.arrays[k] for k in keys]))
        for key, value in zip(keys, held):
            self.arrays[key] = value
        self.flying = []
        made = []
        if layer is not None and self.started >= self.ready[layer]:
            self.gathered[layer] = self.gather(layer)
            made = [self.gathered[layer]]
        if not sends:
            return lax.optimization_barrier((list(through), made))[0]
        choices = [[(names.index(name), index) for name, index in items] for items in chosen.values()]
        shape = (self.each,) + self.weights.shape[2:]
        if self.started == 0:
            picked = [self.weights[0, q * self.each : (q + 1) * self.each] for q in range(2)]
        else:
            picked = pick(self.place, [self.array(n) for n in names], choices, shape)
        for side, array in zip(chosen, picked):
            key = ("got", self.started, side)
            self.arrays[key] = lax.ppermute(array, "pipe", [(p, p ^ side) for p in range(self.square)])
            self.flying.append(key)
        for u, v, piece in sends:
            self.where[v, piece] = ("got", self.started, u ^ v)
        self.started += 1
        return lax.optimization_barrier((list(through), made + list(picked)))[0]

    def gather(self, layer):
        if layer in self.gathered:
            return self.gathered[layer]
        names, plan = [], []
        for q in range(self.parts):
            for p in range(self.square):
                name, index = self.source(p, (layer, q))
                if name not in names:
                    names.append(name)
                plan.append((names.index(name), q * self.each, self.each, index, (1, p)))
        shape = self.weights.shape[1:]
        return gather_weights(self.place, [self.array(name) for name in names], plan, shape)


def gather_square(x):
    mine = lax.axis_index("pipe")
    got = [x] + [lax.ppermute(x, "pipe", [(p, p ^ side) for p in range(4)]) for side in (1, 2, 3)]
    got = jnp.stack(got)
    return jnp.concatenate([lax.dynamic_index_in_dim(got, p ^ mine, 0, keepdims=False) for p in range(4)])


def on_device(features, weights, bias, layout):
    row_devs = lax.axis_size("rows")
    my_row = lax.axis_index("rows")
    neurons = features.shape[1]
    blocks = neurons // BLOCK
    slot_count = blocks * K
    pairs = neurons // LANES
    is_line = row_devs == 4 * CORES and lax.axis_size("pipe") == 4

    mine = lax.dynamic_slice_in_dim(layout, my_row * slot_count, slot_count, axis=1)
    owners, local = mine // blocks, mine % blocks
    table = line_slots(row_devs) if is_line else np.tile(np.arange(row_devs, dtype=np.int32), (row_devs, 1))
    my_slots = lax.dynamic_index_in_dim(jnp.asarray(table), my_row, 0, keepdims=False)
    hit = owners[:, :, None] == jnp.arange(row_devs)[None, None, :]
    slots = jnp.sum(jnp.where(hit, my_slots[None, None, :], 0), axis=2)
    codes = (((slots << bits_for(pairs)) | (local // 2)) << 1) | (local % 2)

    if is_line:
        all_codes, all_bias = gather_square(codes), gather_square(bias)
    else:
        all_codes = lax.all_gather(codes, "pipe", axis=0, tiled=True)
        all_bias = lax.all_gather(bias, "pipe", axis=0, tiled=True)
    z = my_row // CORES
    is_middle = (z > 0) & (z < row_devs // CORES - 1)
    place = jnp.stack([is_middle.astype(jnp.int32), lax.axis_index("pipe").astype(jnp.int32)])
    layers = weights.shape[0] * lax.axis_size("pipe")

    current = features
    if is_line:
        stream = WeightStream(weights, place, 4, WEIGHT_PARTS)
        stream.advance()
        for layer in range(layers):
            step = 0

            def pause(arrived, through):
                nonlocal step, all_codes, all_bias
                step += 1
                if layer == 0 and step == 1:
                    arrived, all_codes, all_bias = lax.optimization_barrier((arrived, all_codes, all_bias))
                return stream.advance([arrived], through, layer if step == 2 else None)

            acts = gather_line(current, pause)
            while stream.started < stream.ready[layer] + (layer == 0):
                stream.advance()
            current = apply_layer(
                all_codes[layer], place, acts, line_plan(), stream.gather(layer), all_bias[layer][None]
            )
        return current

    all_weights = lax.all_gather(weights, "pipe", axis=0, tiled=True)
    for layer in range(layers):
        acts = [lax.all_gather(current, "rows", axis=0, tiled=False)]
        act_plan = [(0, 0, row_devs, None)]
        current = apply_layer(
            all_codes[layer], place, acts, act_plan, all_weights[layer], all_bias[layer][None]
        )
    return current


def solution(mesh):
    in_specs = (
        P("pipe", "rows"),
        P("pipe", "rows", None, None),
        P("pipe", "rows"),
        P("pipe", None),
    )
    out_specs = P("pipe", "rows")
    return jax.shard_map(
        on_device, mesh=mesh, in_specs=in_specs, out_specs=out_specs, check_vma=False
    )
```

```python
import functools
import random

import jax
import jax.numpy as jnp
import numpy as np
from jax import lax
from jax.experimental import pallas as pl
from jax.experimental.pallas import tpu as pltpu
from jax.sharding import PartitionSpec as P

BLOCK = 64
K = 4
LANES = 128
CORES = 2
WEIGHT_PARTS = 4
STREAM_SEED = 486
LAYER_VMEM = 10 * 2**20
SMALL_VMEM = 2 * 2**20

clamp_top = 32.0


def bits_for(count):
    return (count - 1).bit_length()


def start_if(copy, place, want):
    if want is None:
        copy.start()
    else:
        pl.when(place[want[0]] == want[1])(copy.start)


def layer_kernel(act_plan, unroll, codes, place, *refs):
    n_acts = 1 + max(p[0] for p in act_plan)
    acts = refs[:n_acts]
    weights, bias, out, held, masks, act_sem = refs[n_acts:]
    rows = out.shape[0]
    blocks = weights.shape[0]
    pair_bits = bits_for(held.shape[2] // LANES)

    def act_copy(operand, slot, slots):
        src = acts[operand] if slots == 1 else acts[operand].at[:]
        dst = held.at[slot] if slots == 1 else held.at[pl.ds(slot, slots)]
        return pltpu.make_async_copy(src, dst, act_sem.at[slot])

    for operand, slot, slots, want in act_plan:
        start_if(act_copy(operand, slot, slots), place, want)

    low = lax.broadcasted_iota(jnp.int32, (rows, LANES), 1) < BLOCK
    masks[0] = jnp.where(low, 1.0, 0.0).astype(jnp.bfloat16)
    masks[1] = jnp.where(low, 0.0, 1.0).astype(jnp.bfloat16)

    waited = set()
    for operand, slot, slots, _ in act_plan:
        if slot not in waited:
            waited.add(slot)
            act_copy(operand, slot, slots).wait()

    def products(block):
        parts = []
        for k in range(K):
            code = codes[block * K + k]
            pair = (code >> 1) & (2**pair_bits - 1)
            columns = pl.ds(pl.multiple_of(pair * LANES, LANES), LANES)
            parts.append(held[code >> (1 + pair_bits), :, columns] * masks[code & 1])
        left = jnp.concatenate(
            [
                jnp.concatenate([parts[0], parts[2]], axis=1),
                jnp.concatenate([parts[1], parts[3]], axis=1),
            ],
            axis=0,
        )
        w = weights[block]
        first, second = w[:, :LANES], w[:, LANES:]
        right = jnp.concatenate([first, first, second, second], axis=0)
        return jnp.dot(left, right, preferred_element_type=jnp.float32)

    def two_blocks(q, _):
        a, b = products(2 * q), products(2 * q + 1)
        even = a[:rows] + pltpu.roll(a[rows:], BLOCK, 1)
        odd = b[rows:] + pltpu.roll(b[:rows], BLOCK, 1)
        columns = pl.ds(pl.multiple_of(q * LANES, LANES), LANES)
        total = jnp.where(low, even, odd) + bias[:, columns].astype(jnp.float32)
        out[:, columns] = jnp.clip(total, 0.0, clamp_top).astype(jnp.bfloat16)
        return 0

    lax.fori_loop(0, blocks // 2, two_blocks, 0, unroll=min(unroll, blocks // 2))


def gather_weights_kernel(plan, place, *refs):
    sources, out, sem = refs[:-2], refs[-2], refs[-1]

    def copy(operand, first, count, index):
        source = sources[operand] if index is None else sources[operand].at[index]
        return pltpu.make_async_copy(source, out.at[pl.ds(first, count)], sem.at[first])

    for operand, first, count, index, want in plan:
        start_if(copy(operand, first, count, index), place, want)
    for first, (operand, count, index) in {p[1]: (p[0], p[2], p[3]) for p in plan}.items():
        copy(operand, first, count, index).wait()


def pinned(operands, in_hbm):
    return [pltpu.with_memory_space_constraint(x, pltpu.HBM) if n in in_hbm else x for n, x in enumerate(operands)]


def gather_weights(place, weights, in_hbm, plan, shape):
    smem = pl.BlockSpec(memory_space=pltpu.SMEM)
    return pl.pallas_call(
        functools.partial(gather_weights_kernel, plan),
        out_shape=pltpu.VMEM(shape, jnp.bfloat16),
        in_specs=[smem] + [pl.BlockSpec(memory_space=pl.ANY)] * len(weights),
        out_specs=pl.BlockSpec(memory_space=pltpu.VMEM),
        scratch_shapes=[pltpu.SemaphoreType.DMA((shape[0],))],
        compiler_params=pltpu.CompilerParams(vmem_limit_bytes=SMALL_VMEM),
    )(place, *pinned(weights, in_hbm))


def apply_layer(codes, place, acts, act_plan, weights, bias):
    slots = sum(
        count for slot, count in {(slot, count) for _, slot, count, _ in act_plan}
    )
    rows, neurons = acts[0].shape[-2:]
    held = (slots, rows, neurons)
    smem = pl.BlockSpec(memory_space=pltpu.SMEM)
    anywhere = pl.BlockSpec(memory_space=pl.ANY)
    vmem = pl.BlockSpec(memory_space=pltpu.VMEM)
    kernel = functools.partial(layer_kernel, act_plan, 16)
    return pl.pallas_call(
        kernel,
        out_shape=jax.ShapeDtypeStruct((rows, neurons), jnp.bfloat16),
        in_specs=[smem, smem] + [anywhere] * len(acts) + [vmem, vmem],
        out_specs=vmem,
        scratch_shapes=[
            pltpu.VMEM(held, jnp.bfloat16),
            pltpu.VMEM((2, rows, LANES), jnp.bfloat16),
            pltpu.SemaphoreType.DMA((slots,)),
        ],
        compiler_params=pltpu.CompilerParams(vmem_limit_bytes=LAYER_VMEM),
    )(codes, place, *acts, weights, bias)


def along_line(x, pairs):
    moves = [(a * CORES + c, b * CORES + c) for a, b in pairs for c in range(CORES)]
    return lax.ppermute(x, "rows", moves)


def to_other_core(x):
    return lax.ppermute(x, "rows", [(i, i ^ 1) for i in range(lax.axis_size("rows"))])


def after_all(x, *arrived):
    return lax.optimization_barrier((x, *arrived))[0]


def gather_line(x, pause, split):
    inside, ends = [(1, 2), (2, 1)], [(0, 3), (3, 0)]
    near = along_line(x, [(0, 1), (1, 0), (2, 3), (3, 2)])
    cross = along_line(x, inside if split else inside + ends)
    trade = [along_line(x, ends)] if split else []
    x_swapped = to_other_core(x)
    near, cross = pause(x_swapped, [near, cross])
    far = along_line(near, inside)
    outer = along_line(cross, [(2, 3), (1, 0)])
    near_swapped = to_other_core(near)
    (outer,) = pause(near_swapped, [outer])
    rest = [cross, far, outer] + trade
    return [x, near] + rest + [x_swapped, near_swapped] + [to_other_core(buf) for buf in rest]


def line_plan(split):
    middle, ends = (0, 1), (0, 0)
    where = [(0, None), (1, None), (2, middle if split else None), (3, middle), (3, ends), (2, ends)]
    where = where[: 6 if split else 5]
    return [
        (side * len(where) + buf, side * 4 + slot, 1, want)
        for side in range(CORES)
        for buf, (slot, want) in enumerate(where)
    ]


def line_slots(row_devs):
    table = np.zeros((row_devs, row_devs), np.int32)
    chips = row_devs // CORES
    for me in range(row_devs):
        for owner in range(row_devs):
            z, c = divmod(me, CORES)
            oz, oc = divmod(owner, CORES)
            if oz // 2 == z // 2:
                slot = 0 if oz == z else 1
            else:
                across = chips - 1 - z
                slot = 2 if oz == across else 3
            table[me, owner] = (c != oc) * chips + slot
    return table


def stream_order(seed, layers, parts, square):
    draw = random.Random(seed)
    each = layers // square
    links = [(u, u ^ 1) for u in range(square)] + [(u, u ^ 2) for u in range(square)]
    pieces = [(layer, q) for layer in range(layers) for q in range(parts)]
    have = {(p, piece): 0 for p in range(square) for piece in pieces if piece[0] // each == p}
    noise, direct, spread = draw.choice([0, 0.3, 1, 2]), draw.choice([0, 1, 2]), draw.choice([0, 0.5, 1, 2])
    slots = []
    while len(have) < square * len(pieces):
        now, sends = len(slots), []
        taken = set()
        order = links[:]
        draw.shuffle(order)
        if now == 0:
            sends = [(u, v, (u * each, 0 if u ^ v == 1 else 1)) for u, v in links]
            order = []
        for u, v in order:
            best = None
            for piece in pieces:
                if (v, piece) in have or (v, piece) in taken or have.get((u, piece), now + 1) > now:
                    continue
                w = v ^ 1 if u == v ^ 2 else v ^ 2
                holders = sum((p, piece) in have or (p, piece) in taken for p in range(square))
                also = have.get((w, piece), now + 1) <= now
                key = piece[0] * 4 + direct * also + spread * holders + noise * draw.random()
                if best is None or key < best[0]:
                    best = (key, piece)
            if best is not None:
                taken.add((v, best[1]))
                sends.append((u, v, best[1]))
        for u, v, piece in sends:
            have[v, piece] = now + 1
        slots.append(sends)
    ready = [max(have[p, (layer, q)] for p in range(square) for q in range(parts)) for layer in range(layers)]
    return slots, ready


def pick_kernel(choices, count, place, *refs):
    sources, outs, sems = refs[:-count - 1], refs[-count - 1 : -1], refs[-1]

    def copy_for(p):
        copies = []
        for n, per_device in enumerate(choices):
            operand, index = per_device[p]
            source = sources[operand] if index is None else sources[operand].at[index]
            copies.append(pltpu.make_async_copy(source, outs[n], sems.at[n]))
        for copy in copies:
            copy.start()
        for copy in copies:
            copy.wait()

    for p in range(len(choices[0])):
        pl.when(place[1] == p)(functools.partial(copy_for, p))


def pick(place, operands, in_hbm, choices, shape):
    smem = pl.BlockSpec(memory_space=pltpu.SMEM)
    return pl.pallas_call(
        functools.partial(pick_kernel, choices, len(choices)),
        out_shape=[pltpu.VMEM(shape, jnp.bfloat16)] * len(choices),
        in_specs=[smem] + [pl.BlockSpec(memory_space=pl.ANY)] * len(operands),
        out_specs=[pl.BlockSpec(memory_space=pltpu.VMEM)] * len(choices),
        scratch_shapes=[pltpu.SemaphoreType.DMA((len(choices),))],
        compiler_params=pltpu.CompilerParams(vmem_limit_bytes=SMALL_VMEM),
    )(place, *pinned(operands, in_hbm))


def load_kernel(source, out, sem):
    copy = pltpu.make_async_copy(source, out, sem)
    copy.start()
    copy.wait()


def load(x):
    return pl.pallas_call(
        load_kernel,
        out_shape=pltpu.VMEM(x.shape, x.dtype),
        in_specs=[pl.BlockSpec(memory_space=pl.ANY)],
        out_specs=pl.BlockSpec(memory_space=pltpu.VMEM),
        scratch_shapes=[pltpu.SemaphoreType.DMA],
        compiler_params=pltpu.CompilerParams(vmem_limit_bytes=SMALL_VMEM),
    )(pltpu.with_memory_space_constraint(x, pltpu.HBM))


class WeightStream:
    def __init__(self, weights, place, square, parts):
        self.weights, self.place = weights, place
        self.sections, self.parts = weights.shape[0], parts
        self.each = weights.shape[1] // parts
        self.slots, self.ready = stream_order(STREAM_SEED, square * self.sections, parts, square)
        self.square = square
        self.arrays = {}
        self.where = {}
        self.flying = []
        self.loaded = False
        self.started = 0
        self.gathered = {}

    def source(self, p, piece):
        if piece is None:
            piece = (p * self.sections, 0)
        if (p, piece) in self.where:
            return self.where[p, piece], None
        return "own", (piece[0] % self.sections, pl.ds(piece[1] * self.each, self.each))

    def array(self, name):
        return self.weights if name == "own" else self.arrays[name]

    def advance(self, after=(), through=()):
        sends = self.slots[self.started] if self.started < len(self.slots) else []
        sides = {}
        for u, v, piece in sends:
            sides.setdefault(u ^ v, {})[u] = piece
        chosen = {side: [self.source(p, by.get(p)) for p in range(self.square)] for side, by in sorted(sides.items())}
        names = sorted({name for items in chosen.values() for name, _ in items}, key=str)
        keys = self.flying + [n for n in names if n != "own" and n not in self.flying]
        _, held = lax.optimization_barrier((list(after), [self.arrays[k] for k in keys]))
        for key, value in zip(keys, held):
            self.arrays[key] = value
        self.flying = []
        if not sends:
            return list(through)
        choices = [[(names.index(name), index) for name, index in items] for items in chosen.values()]
        shape = (self.each,) + self.weights.shape[2:]
        in_hbm = [n for n, name in enumerate(names) if name == "own" and not self.loaded]
        picked = pick(self.place, [self.array(n) for n in names], in_hbm, choices, shape)
        for side, array in zip(chosen, picked):
            key = ("got", self.started, side)
            self.arrays[key] = lax.ppermute(array, "pipe", [(p, p ^ side) for p in range(self.square)])
            self.flying.append(key)
        for u, v, piece in sends:
            self.where[v, piece] = ("got", self.started, u ^ v)
        self.started += 1
        return lax.optimization_barrier((list(through), picked))[0]

    def gather(self, layer):
        if layer in self.gathered:
            return self.gathered[layer]
        names, plan = [], []
        for q in range(self.parts):
            for p in range(self.square):
                name, index = self.source(p, (layer, q))
                if name not in names:
                    names.append(name)
                plan.append((names.index(name), q * self.each, self.each, index, (1, p)))
        in_hbm = [n for n, name in enumerate(names) if name == "own" and not self.loaded]
        arrays = [self.array(name) for name in names]
        self.gathered[layer] = gather_weights(self.place, arrays, in_hbm, plan, self.weights.shape[1:])
        return self.gathered[layer]


def gather_square(x):
    mine = lax.axis_index("pipe")
    got = [x] + [lax.ppermute(x, "pipe", [(p, p ^ side) for p in range(4)]) for side in (1, 2, 3)]
    got = jnp.stack(got)
    return jnp.concatenate([lax.dynamic_index_in_dim(got, p ^ mine, 0, keepdims=False) for p in range(4)])


def on_device(features, weights, bias, layout):
    row_devs = lax.axis_size("rows")
    my_row = lax.axis_index("rows")
    neurons = features.shape[1]
    blocks = neurons // BLOCK
    slot_count = blocks * K
    pairs = neurons // LANES
    is_line = row_devs == 4 * CORES and lax.axis_size("pipe") == 4

    mine = lax.dynamic_slice_in_dim(layout, my_row * slot_count, slot_count, axis=1)
    owners, local = mine // blocks, mine % blocks
    table = line_slots(row_devs) if is_line else np.tile(np.arange(row_devs, dtype=np.int32), (row_devs, 1))
    my_slots = lax.dynamic_index_in_dim(jnp.asarray(table), my_row, 0, keepdims=False)
    hit = owners[:, :, None] == jnp.arange(row_devs)[None, None, :]
    slots = jnp.sum(jnp.where(hit, my_slots[None, None, :], 0), axis=2)
    codes = (((slots << bits_for(pairs)) | (local // 2)) << 1) | (local % 2)

    if is_line:
        all_codes, all_bias = gather_square(codes), gather_square(bias)
    else:
        all_codes = lax.all_gather(codes, "pipe", axis=0, tiled=True)
        all_bias = lax.all_gather(bias, "pipe", axis=0, tiled=True)
    z = my_row // CORES
    is_middle = (z > 0) & (z < row_devs // CORES - 1)
    place = jnp.stack([is_middle.astype(jnp.int32), lax.axis_index("pipe").astype(jnp.int32)])
    layers = weights.shape[0] * lax.axis_size("pipe")

    current = features
    if is_line:
        stream = WeightStream(weights, place, 4, WEIGHT_PARTS)
        stream.advance()
        for layer in range(layers):
            step = 0

            def pause(arrived, through):
                nonlocal step
                step += 1
                if layer == 0 and step == 1:
                    stream.weights = load(after_all(weights, arrived))
                    stream.loaded = True
                if step == 1:
                    through = stream.advance([arrived] + ([all_codes, all_bias] if layer == 0 else []), through)
                else:
                    through = stream.advance([arrived], through)
                if step == 2 and stream.started >= stream.ready[layer]:
                    through, _ = lax.optimization_barrier((through, stream.gather(layer)))
                return through

            split = stream.started == len(stream.slots)
            acts = gather_line(current, pause, split)
            while stream.started < stream.ready[layer] + (layer == 0):
                stream.advance()
            current = apply_layer(
                all_codes[layer], place, acts, line_plan(split), stream.gather(layer), all_bias[layer][None]
            )
        return current

    all_weights = lax.all_gather(weights, "pipe", axis=0, tiled=True)
    for layer in range(layers):
        acts = [lax.all_gather(current, "rows", axis=0, tiled=False)]
        act_plan = [(0, 0, row_devs, None)]
        current = apply_layer(
            all_codes[layer], place, acts, act_plan, all_weights[layer], all_bias[layer][None]
        )
    return current


def solution(mesh):
    in_specs = (
        P("pipe", "rows"),
        P("pipe", "rows", None, None),
        P("pipe", "rows"),
        P("pipe", None),
    )
    out_specs = P("pipe", "rows")
    return jax.shard_map(
        on_device, mesh=mesh, in_specs=in_specs, out_specs=out_specs, check_vma=False
    )
```

```python
import functools
import random

import jax
import jax.numpy as jnp
import numpy as np
from jax import lax
from jax.experimental import pallas as pl
from jax.experimental.pallas import tpu as pltpu
from jax.sharding import PartitionSpec as P

BLOCK = 64
K = 4
LANES = 128
CORES = 2
WEIGHT_PARTS = 4
STREAM_SEED = 486
BUSY_LAYERS = (0, 1, 3, 4)
LAYER_VMEM = 10 * 2**20
SMALL_VMEM = 2 * 2**20
BRIEF = pl.CostEstimate(flops=0, transcendentals=0, bytes_accessed=0)

clamp_top = 32.0


def bits_for(count):
    return (count - 1).bit_length()


def start_if(copy, place, want):
    if want is None:
        copy.start()
    else:
        pl.when(place[want[0]] == want[1])(copy.start)


def layer_kernel(act_plan, unroll, codes, place, *refs):
    n_acts = 1 + max(p[0] for p in act_plan)
    acts = refs[:n_acts]
    weights, bias, out, held, masks, act_sem = refs[n_acts:]
    rows = out.shape[0]
    blocks = weights.shape[0]
    pair_bits = bits_for(held.shape[2] // LANES)

    def act_copy(operand, slot, slots):
        src = acts[operand] if slots == 1 else acts[operand].at[:]
        dst = held.at[slot] if slots == 1 else held.at[pl.ds(slot, slots)]
        return pltpu.make_async_copy(src, dst, act_sem.at[slot])

    for operand, slot, slots, want in act_plan:
        start_if(act_copy(operand, slot, slots), place, want)

    low = lax.broadcasted_iota(jnp.int32, (rows, LANES), 1) < BLOCK
    masks[0] = jnp.where(low, 1.0, 0.0).astype(jnp.bfloat16)
    masks[1] = jnp.where(low, 0.0, 1.0).astype(jnp.bfloat16)

    waited = set()
    for operand, slot, slots, _ in act_plan:
        if slot not in waited:
            waited.add(slot)
            act_copy(operand, slot, slots).wait()

    def products(block):
        parts = []
        for k in range(K):
            code = codes[block * K + k]
            pair = (code >> 1) & (2**pair_bits - 1)
            columns = pl.ds(pl.multiple_of(pair * LANES, LANES), LANES)
            parts.append(held[code >> (1 + pair_bits), :, columns] * masks[code & 1])
        left = jnp.concatenate(
            [
                jnp.concatenate([parts[0], parts[2]], axis=1),
                jnp.concatenate([parts[1], parts[3]], axis=1),
            ],
            axis=0,
        )
        w = weights[block]
        first, second = w[:, :LANES], w[:, LANES:]
        right = jnp.concatenate([first, first, second, second], axis=0)
        return jnp.dot(left, right, preferred_element_type=jnp.float32)

    def two_blocks(q, _):
        a, b = products(2 * q), products(2 * q + 1)
        even = a[:rows] + pltpu.roll(a[rows:], BLOCK, 1)
        odd = b[rows:] + pltpu.roll(b[:rows], BLOCK, 1)
        columns = pl.ds(pl.multiple_of(q * LANES, LANES), LANES)
        total = jnp.where(low, even, odd) + bias[:, columns].astype(jnp.float32)
        out[:, columns] = jnp.clip(total, 0.0, clamp_top).astype(jnp.bfloat16)
        return 0

    lax.fori_loop(0, blocks // 2, two_blocks, 0, unroll=min(unroll, blocks // 2))


def gather_weights_kernel(plan, place, *refs):
    sources, out, sem = refs[:-2], refs[-2], refs[-1]

    def copy(operand, first, count, index):
        source = sources[operand] if index is None else sources[operand].at[index]
        return pltpu.make_async_copy(source, out.at[pl.ds(first, count)], sem.at[first])

    for operand, first, count, index, want in plan:
        start_if(copy(operand, first, count, index), place, want)
    for first, (operand, count, index) in {p[1]: (p[0], p[2], p[3]) for p in plan}.items():
        copy(operand, first, count, index).wait()


def pinned(operands, in_hbm):
    return [pltpu.with_memory_space_constraint(x, pltpu.HBM) if n in in_hbm else x for n, x in enumerate(operands)]


def gather_weights(place, weights, in_hbm, plan, shape):
    smem = pl.BlockSpec(memory_space=pltpu.SMEM)
    return pl.pallas_call(
        functools.partial(gather_weights_kernel, plan),
        out_shape=pltpu.VMEM(shape, jnp.bfloat16),
        in_specs=[smem] + [pl.BlockSpec(memory_space=pl.ANY)] * len(weights),
        out_specs=pl.BlockSpec(memory_space=pltpu.VMEM),
        scratch_shapes=[pltpu.SemaphoreType.DMA((shape[0],))],
        cost_estimate=BRIEF,
        compiler_params=pltpu.CompilerParams(vmem_limit_bytes=SMALL_VMEM),
    )(place, *pinned(weights, in_hbm))


def apply_layer(codes, place, acts, act_plan, weights, bias):
    slots = sum(
        count for slot, count in {(slot, count) for _, slot, count, _ in act_plan}
    )
    rows, neurons = acts[0].shape[-2:]
    held = (slots, rows, neurons)
    smem = pl.BlockSpec(memory_space=pltpu.SMEM)
    anywhere = pl.BlockSpec(memory_space=pl.ANY)
    vmem = pl.BlockSpec(memory_space=pltpu.VMEM)
    kernel = functools.partial(layer_kernel, act_plan, 64)
    return pl.pallas_call(
        kernel,
        out_shape=jax.ShapeDtypeStruct((rows, neurons), jnp.bfloat16),
        in_specs=[smem, smem] + [anywhere] * len(acts) + [vmem, vmem],
        out_specs=vmem,
        scratch_shapes=[
            pltpu.VMEM(held, jnp.bfloat16),
            pltpu.VMEM((2, rows, LANES), jnp.bfloat16),
            pltpu.SemaphoreType.DMA((slots,)),
        ],
        cost_estimate=BRIEF,
        compiler_params=pltpu.CompilerParams(vmem_limit_bytes=LAYER_VMEM),
    )(codes, place, *acts, weights, bias)


def along_line(x, pairs):
    moves = [(a * CORES + c, b * CORES + c) for a, b in pairs for c in range(CORES)]
    return lax.ppermute(x, "rows", moves)


def to_other_core(x):
    return lax.ppermute(x, "rows", [(i, i ^ 1) for i in range(lax.axis_size("rows"))])


def after_all(x, *arrived):
    return lax.optimization_barrier((x, *arrived))[0]


def gather_line(x, pause, split):
    inside, ends = [(1, 2), (2, 1)], [(0, 3), (3, 0)]
    near = along_line(x, [(0, 1), (1, 0), (2, 3), (3, 2)])
    cross = along_line(x, inside if split else inside + ends)
    trade = [along_line(x, ends)] if split else []
    x_swapped = to_other_core(x)
    near, cross = pause([x_swapped], [near, cross])
    far = along_line(near, inside)
    outer = along_line(cross, [(2, 3), (1, 0)])
    near_swapped, cross_swapped = to_other_core(near), to_other_core(cross)
    far, outer = pause([near_swapped, cross_swapped], [far, outer])
    rest = [far, outer] + trade
    swapped = [x_swapped, near_swapped, cross_swapped] + [to_other_core(buf) for buf in rest]
    return [x, near, cross] + rest + swapped


def line_plan(split):
    middle, ends = (0, 1), (0, 0)
    where = [(0, None), (1, None), (2, middle if split else None), (3, middle), (3, ends), (2, ends)]
    where = where[: 6 if split else 5]
    return [
        (side * len(where) + buf, side * 4 + slot, 1, want)
        for side in range(CORES)
        for buf, (slot, want) in enumerate(where)
    ]


def line_slots(row_devs):
    table = np.zeros((row_devs, row_devs), np.int32)
    chips = row_devs // CORES
    for me in range(row_devs):
        for owner in range(row_devs):
            z, c = divmod(me, CORES)
            oz, oc = divmod(owner, CORES)
            if oz // 2 == z // 2:
                slot = 0 if oz == z else 1
            else:
                across = chips - 1 - z
                slot = 2 if oz == across else 3
            table[me, owner] = (c != oc) * chips + slot
    return table


def stream_order(seed, layers, parts, square):
    draw = random.Random(seed)
    each = layers // square
    links = [(u, u ^ 1) for u in range(square)] + [(u, u ^ 2) for u in range(square)]
    pieces = [(layer, q) for layer in range(layers) for q in range(parts)]
    have = {(p, piece): 0 for p in range(square) for piece in pieces if piece[0] // each == p}
    noise, direct, spread = draw.choice([0, 0.3, 1, 2]), draw.choice([0, 1, 2]), draw.choice([0, 0.5, 1, 2])
    slots = []
    while len(have) < square * len(pieces):
        now, sends = len(slots), []
        taken = set()
        order = links[:]
        draw.shuffle(order)
        if now == 0:
            sends = [(u, v, (u * each, 0 if u ^ v == 1 else 1)) for u, v in links]
            order = []
        for u, v in order:
            best = None
            for piece in pieces:
                if (v, piece) in have or (v, piece) in taken or have.get((u, piece), now + 1) > now:
                    continue
                w = v ^ 1 if u == v ^ 2 else v ^ 2
                holders = sum((p, piece) in have or (p, piece) in taken for p in range(square))
                also = have.get((w, piece), now + 1) <= now
                key = piece[0] * 4 + direct * also + spread * holders + noise * draw.random()
                if best is None or key < best[0]:
                    best = (key, piece)
            if best is not None:
                taken.add((v, best[1]))
                sends.append((u, v, best[1]))
        for u, v, piece in sends:
            have[v, piece] = now + 1
        slots.append(sends)
    ready = [max(have[p, (layer, q)] for p in range(square) for q in range(parts)) for layer in range(layers)]
    return slots, ready


def pick_kernel(choices, count, place, *refs):
    sources, outs, sems = refs[:-count - 1], refs[-count - 1 : -1], refs[-1]

    def copy_for(p):
        copies = []
        for n, per_device in enumerate(choices):
            operand, index = per_device[p]
            source = sources[operand] if index is None else sources[operand].at[index]
            copies.append(pltpu.make_async_copy(source, outs[n], sems.at[n]))
        for copy in copies:
            copy.start()
        for copy in copies:
            copy.wait()

    for p in range(len(choices[0])):
        pl.when(place[1] == p)(functools.partial(copy_for, p))


def pick(place, operands, in_hbm, choices, shape):
    smem = pl.BlockSpec(memory_space=pltpu.SMEM)
    return pl.pallas_call(
        functools.partial(pick_kernel, choices, len(choices)),
        out_shape=[pltpu.VMEM(shape, jnp.bfloat16)] * len(choices),
        in_specs=[smem] + [pl.BlockSpec(memory_space=pl.ANY)] * len(operands),
        out_specs=[pl.BlockSpec(memory_space=pltpu.VMEM)] * len(choices),
        scratch_shapes=[pltpu.SemaphoreType.DMA((len(choices),))],
        cost_estimate=BRIEF,
        compiler_params=pltpu.CompilerParams(vmem_limit_bytes=SMALL_VMEM),
    )(place, *pinned(operands, in_hbm))


def load_kernel(source, out, sem):
    copy = pltpu.make_async_copy(source, out, sem)
    copy.start()
    copy.wait()


def load(x):
    return pl.pallas_call(
        load_kernel,
        out_shape=pltpu.VMEM(x.shape, x.dtype),
        in_specs=[pl.BlockSpec(memory_space=pl.ANY)],
        out_specs=pl.BlockSpec(memory_space=pltpu.VMEM),
        scratch_shapes=[pltpu.SemaphoreType.DMA],
        cost_estimate=BRIEF,
        compiler_params=pltpu.CompilerParams(vmem_limit_bytes=SMALL_VMEM),
    )(pltpu.with_memory_space_constraint(x, pltpu.HBM))


class WeightStream:
    def __init__(self, weights, place, square, parts):
        self.weights, self.place = weights, place
        self.sections, self.parts = weights.shape[0], parts
        self.each = weights.shape[1] // parts
        self.slots, self.ready = stream_order(STREAM_SEED, square * self.sections, parts, square)
        self.square = square
        self.arrays = {}
        self.where = {}
        self.flying = []
        self.loaded = False
        self.started = 0
        self.gathered = {}

    def source(self, p, piece):
        if piece is None:
            piece = (p * self.sections, 0)
        if (p, piece) in self.where:
            return self.where[p, piece], None
        return "own", (piece[0] % self.sections, pl.ds(piece[1] * self.each, self.each))

    def array(self, name):
        return self.weights if name == "own" else self.arrays[name]

    def advance(self, after=(), through=()):
        sends = self.slots[self.started] if self.started < len(self.slots) else []
        sides = {}
        for u, v, piece in sends:
            sides.setdefault(u ^ v, {})[u] = piece
        chosen = {side: [self.source(p, by.get(p)) for p in range(self.square)] for side, by in sorted(sides.items())}
        names = sorted({name for items in chosen.values() for name, _ in items}, key=str)
        keys = self.flying + [n for n in names if n != "own" and n not in self.flying]
        _, held = lax.optimization_barrier((list(after), [self.arrays[k] for k in keys]))
        for key, value in zip(keys, held):
            self.arrays[key] = value
        self.flying = []
        if not sends:
            return list(through)
        choices = [[(names.index(name), index) for name, index in items] for items in chosen.values()]
        shape = (self.each,) + self.weights.shape[2:]
        in_hbm = [n for n, name in enumerate(names) if name == "own" and not self.loaded]
        picked = pick(self.place, [self.array(n) for n in names], in_hbm, choices, shape)
        for side, array in zip(chosen, picked):
            key = ("got", self.started, side)
            self.arrays[key] = lax.ppermute(array, "pipe", [(p, p ^ side) for p in range(self.square)])
            self.flying.append(key)
        for u, v, piece in sends:
            self.where[v, piece] = ("got", self.started, u ^ v)
        self.started += 1
        return lax.optimization_barrier((list(through), picked))[0]

    def gather(self, layer):
        if layer in self.gathered:
            return self.gathered[layer]
        names, plan = [], []
        for q in range(self.parts):
            for p in range(self.square):
                name, index = self.source(p, (layer, q))
                if name not in names:
                    names.append(name)
                plan.append((names.index(name), q * self.each, self.each, index, (1, p)))
        in_hbm = [n for n, name in enumerate(names) if name == "own" and not self.loaded]
        arrays = [self.array(name) for name in names]
        self.gathered[layer] = gather_weights(self.place, arrays, in_hbm, plan, self.weights.shape[1:])
        return self.gathered[layer]


def gather_square(x):
    mine = lax.axis_index("pipe")
    got = [x] + [lax.ppermute(x, "pipe", [(p, p ^ side) for p in range(4)]) for side in (1, 2, 3)]
    got = jnp.stack(got)
    return jnp.concatenate([lax.dynamic_index_in_dim(got, p ^ mine, 0, keepdims=False) for p in range(4)])


def on_device(features, weights, bias, layout):
    row_devs = lax.axis_size("rows")
    my_row = lax.axis_index("rows")
    neurons = features.shape[1]
    blocks = neurons // BLOCK
    slot_count = blocks * K
    pairs = neurons // LANES
    is_line = row_devs == 4 * CORES and lax.axis_size("pipe") == 4

    z = my_row // CORES
    is_middle = (z > 0) & (z < row_devs // CORES - 1)
    place = jnp.stack([is_middle.astype(jnp.int32), lax.axis_index("pipe").astype(jnp.int32)])
    if is_line:
        stream = WeightStream(weights, place, 4, WEIGHT_PARTS)
        layout, bias = stream.advance(through=[layout, bias])

    mine = lax.dynamic_slice_in_dim(layout, my_row * slot_count, slot_count, axis=1)
    owners, local = mine // blocks, mine % blocks
    table = line_slots(row_devs) if is_line else np.tile(np.arange(row_devs, dtype=np.int32), (row_devs, 1))
    my_slots = lax.dynamic_index_in_dim(jnp.asarray(table), my_row, 0, keepdims=False)
    hit = owners[:, :, None] == jnp.arange(row_devs)[None, None, :]
    slots = jnp.sum(jnp.where(hit, my_slots[None, None, :], 0), axis=2)
    codes = (((slots << bits_for(pairs)) | (local // 2)) << 1) | (local % 2)

    if is_line:
        base = 2 ** (bits_for(4 * CORES * pairs * 2) // 2)
        sent = jnp.concatenate([bias, *(part.astype(jnp.bfloat16) for part in (codes // base, codes % base))], axis=1)
        got = gather_square(sent)
        high, low = (
            got[:, neurons + n * slot_count : neurons + (n + 1) * slot_count].astype(jnp.int32) for n in range(2)
        )
        all_codes, all_bias = high * base + low, got[:, :neurons]
    else:
        all_codes = lax.all_gather(codes, "pipe", axis=0, tiled=True)
        all_bias = lax.all_gather(bias, "pipe", axis=0, tiled=True)
    layers = weights.shape[0] * lax.axis_size("pipe")

    current = features
    if is_line:
        for layer in range(layers):
            step = 0

            def pause(arrived, through):
                nonlocal step
                step += 1
                if layer == 0 and step == 1:
                    stream.weights = load(after_all(weights, *arrived))
                    stream.loaded = True
                if step == 1:
                    through = stream.advance(arrived + ([all_codes, all_bias] if layer == 0 else []), through)
                elif layer in BUSY_LAYERS:
                    through = stream.advance(arrived, through)
                if step == 2 and stream.started >= stream.ready[layer]:
                    through, _ = lax.optimization_barrier((through, stream.gather(layer)))
                return through

            split = stream.started == len(stream.slots)
            acts = gather_line(current, pause, split)
            while stream.started < stream.ready[layer] + (layer == 0):
                stream.advance()
            current = apply_layer(
                all_codes[layer], place, acts, line_plan(split), stream.gather(layer), all_bias[layer][None]
            )
        return current

    all_weights = lax.all_gather(weights, "pipe", axis=0, tiled=True)
    for layer in range(layers):
        acts = [lax.all_gather(current, "rows", axis=0, tiled=False)]
        act_plan = [(0, 0, row_devs, None)]
        current = apply_layer(
            all_codes[layer], place, acts, act_plan, all_weights[layer], all_bias[layer][None]
        )
    return current


def solution(mesh):
    in_specs = (
        P("pipe", "rows"),
        P("pipe", "rows", None, None),
        P("pipe", "rows"),
        P("pipe", None),
    )
    out_specs = P("pipe", "rows")
    return jax.shard_map(
        on_device, mesh=mesh, in_specs=in_specs, out_specs=out_specs, check_vma=False
    )
```

```python
import functools
import random

import jax
import jax.numpy as jnp
import numpy as np
from jax import lax
from jax.experimental import pallas as pl
from jax.experimental.pallas import tpu as pltpu
from jax.sharding import PartitionSpec as P

BLOCK = 64
K = 4
LANES = 128
CORES = 2
WEIGHT_PARTS = 4
STREAM_SEED = 486
BUSY_LAYERS = (0, 1, 3, 4)
LAYER_VMEM = 10 * 2**20
SMALL_VMEM = 2 * 2**20
BRIEF = pl.CostEstimate(flops=0, transcendentals=0, bytes_accessed=0)

clamp_top = 32.0


def bits_for(count):
    return (count - 1).bit_length()


def start_if(copy, place, want):
    if want is None:
        copy.start()
    else:
        pl.when(place[want[0]] == want[1])(copy.start)


def layer_kernel(act_plan, unroll, codes, place, *refs):
    n_acts = 1 + max(p[0] for p in act_plan)
    acts = refs[:n_acts]
    weights, bias, out, held, masks, act_sem = refs[n_acts:]
    rows = out.shape[0]
    blocks = weights.shape[0]
    pair_bits = bits_for(held.shape[2] // LANES)

    def act_copy(operand, slot, slots):
        src = acts[operand] if slots == 1 else acts[operand].at[:]
        dst = held.at[slot] if slots == 1 else held.at[pl.ds(slot, slots)]
        return pltpu.make_async_copy(src, dst, act_sem.at[slot])

    for operand, slot, slots, want in act_plan:
        start_if(act_copy(operand, slot, slots), place, want)

    low = lax.broadcasted_iota(jnp.int32, (rows, LANES), 1) < BLOCK
    masks[0] = jnp.where(low, 1.0, 0.0).astype(jnp.bfloat16)
    masks[1] = jnp.where(low, 0.0, 1.0).astype(jnp.bfloat16)

    waited = set()
    for operand, slot, slots, _ in act_plan:
        if slot not in waited:
            waited.add(slot)
            act_copy(operand, slot, slots).wait()

    def products(block):
        parts = []
        for k in range(K):
            code = codes[block * K + k]
            pair = (code >> 1) & (2**pair_bits - 1)
            columns = pl.ds(pl.multiple_of(pair * LANES, LANES), LANES)
            parts.append(held[code >> (1 + pair_bits), :, columns] * masks[code & 1])
        left = jnp.concatenate(
            [
                jnp.concatenate([parts[0], parts[2]], axis=1),
                jnp.concatenate([parts[1], parts[3]], axis=1),
            ],
            axis=0,
        )
        w = weights[block]
        first, second = w[:, :LANES], w[:, LANES:]
        right = jnp.concatenate([first, first, second, second], axis=0)
        return jnp.dot(left, right, preferred_element_type=jnp.float32)

    def two_blocks(q, _):
        a, b = products(2 * q), products(2 * q + 1)
        even = a[:rows] + pltpu.roll(a[rows:], BLOCK, 1)
        odd = b[rows:] + pltpu.roll(b[:rows], BLOCK, 1)
        columns = pl.ds(pl.multiple_of(q * LANES, LANES), LANES)
        total = jnp.where(low, even, odd) + bias[:, columns].astype(jnp.float32)
        out[:, columns] = jnp.clip(total, 0.0, clamp_top).astype(jnp.bfloat16)
        return 0

    lax.fori_loop(0, blocks // 2, two_blocks, 0, unroll=min(unroll, blocks // 2))


def gather_weights_kernel(plan, place, *refs):
    sources, out, sem = refs[:-2], refs[-2], refs[-1]

    def copy(operand, first, count, index):
        source = sources[operand] if index is None else sources[operand].at[index]
        return pltpu.make_async_copy(source, out.at[pl.ds(first, count)], sem.at[first])

    for operand, first, count, index, want in plan:
        start_if(copy(operand, first, count, index), place, want)
    for first, (operand, count, index) in {p[1]: (p[0], p[2], p[3]) for p in plan}.items():
        copy(operand, first, count, index).wait()


def pinned(operands, in_hbm):
    return [pltpu.with_memory_space_constraint(x, pltpu.HBM) if n in in_hbm else x for n, x in enumerate(operands)]


def gather_weights(place, weights, in_hbm, plan, shape):
    smem = pl.BlockSpec(memory_space=pltpu.SMEM)
    return pl.pallas_call(
        functools.partial(gather_weights_kernel, plan),
        out_shape=pltpu.VMEM(shape, jnp.bfloat16),
        in_specs=[smem] + [pl.BlockSpec(memory_space=pl.ANY)] * len(weights),
        out_specs=pl.BlockSpec(memory_space=pltpu.VMEM),
        scratch_shapes=[pltpu.SemaphoreType.DMA((shape[0],))],
        cost_estimate=BRIEF,
        compiler_params=pltpu.CompilerParams(vmem_limit_bytes=SMALL_VMEM),
    )(place, *pinned(weights, in_hbm))


def apply_layer(codes, place, acts, act_plan, weights, bias):
    slots = sum(
        count for slot, count in {(slot, count) for _, slot, count, _ in act_plan}
    )
    rows, neurons = acts[0].shape[-2:]
    held = (slots, rows, neurons)
    smem = pl.BlockSpec(memory_space=pltpu.SMEM)
    anywhere = pl.BlockSpec(memory_space=pl.ANY)
    vmem = pl.BlockSpec(memory_space=pltpu.VMEM)
    kernel = functools.partial(layer_kernel, act_plan, 16)
    return pl.pallas_call(
        kernel,
        out_shape=jax.ShapeDtypeStruct((rows, neurons), jnp.bfloat16),
        in_specs=[smem, smem] + [anywhere] * len(acts) + [vmem, vmem],
        out_specs=vmem,
        scratch_shapes=[
            pltpu.VMEM(held, jnp.bfloat16),
            pltpu.VMEM((2, rows, LANES), jnp.bfloat16),
            pltpu.SemaphoreType.DMA((slots,)),
        ],
        cost_estimate=BRIEF,
        compiler_params=pltpu.CompilerParams(vmem_limit_bytes=LAYER_VMEM),
    )(codes, place, *acts, weights, bias)


def along_line(x, pairs):
    moves = [(a * CORES + c, b * CORES + c) for a, b in pairs for c in range(CORES)]
    return lax.ppermute(x, "rows", moves)


def to_other_core(x):
    return lax.ppermute(x, "rows", [(i, i ^ 1) for i in range(lax.axis_size("rows"))])


def after_all(x, *arrived):
    return lax.optimization_barrier((x, *arrived))[0]


def gather_line(x, pause, split):
    inside, ends = [(1, 2), (2, 1)], [(0, 3), (3, 0)]
    near = along_line(x, [(0, 1), (1, 0), (2, 3), (3, 2)])
    cross = along_line(x, inside if split else inside + ends)
    trade = [along_line(x, ends)] if split else []
    x_swapped = to_other_core(x)
    near, cross = pause([x_swapped], [near, cross])
    far = along_line(near, inside)
    outer = along_line(cross, [(2, 3), (1, 0)])
    near_swapped, cross_swapped = to_other_core(near), to_other_core(cross)
    far, outer = pause([near_swapped, cross_swapped], [far, outer])
    rest = [far, outer] + trade
    swapped = [x_swapped, near_swapped, cross_swapped] + [to_other_core(buf) for buf in rest]
    return [x, near, cross] + rest + swapped


def line_plan(split):
    middle, ends = (0, 1), (0, 0)
    where = [(0, None), (1, None), (2, middle if split else None), (3, middle), (3, ends), (2, ends)]
    where = where[: 6 if split else 5]
    return [
        (side * len(where) + buf, side * 4 + slot, 1, want)
        for side in range(CORES)
        for buf, (slot, want) in enumerate(where)
    ]


def line_slots(row_devs):
    table = np.zeros((row_devs, row_devs), np.int32)
    chips = row_devs // CORES
    for me in range(row_devs):
        for owner in range(row_devs):
            z, c = divmod(me, CORES)
            oz, oc = divmod(owner, CORES)
            if oz // 2 == z // 2:
                slot = 0 if oz == z else 1
            else:
                across = chips - 1 - z
                slot = 2 if oz == across else 3
            table[me, owner] = (c != oc) * chips + slot
    return table


def stream_order(seed, layers, parts, square):
    draw = random.Random(seed)
    each = layers // square
    links = [(u, u ^ 1) for u in range(square)] + [(u, u ^ 2) for u in range(square)]
    pieces = [(layer, q) for layer in range(layers) for q in range(parts)]
    have = {(p, piece): 0 for p in range(square) for piece in pieces if piece[0] // each == p}
    noise, direct, spread = draw.choice([0, 0.3, 1, 2]), draw.choice([0, 1, 2]), draw.choice([0, 0.5, 1, 2])
    slots = []
    while len(have) < square * len(pieces):
        now, sends = len(slots), []
        taken = set()
        order = links[:]
        draw.shuffle(order)
        if now == 0:
            sends = [(u, v, (u * each, 0 if u ^ v == 1 else 1)) for u, v in links]
            order = []
        for u, v in order:
            best = None
            for piece in pieces:
                if (v, piece) in have or (v, piece) in taken or have.get((u, piece), now + 1) > now:
                    continue
                w = v ^ 1 if u == v ^ 2 else v ^ 2
                holders = sum((p, piece) in have or (p, piece) in taken for p in range(square))
                also = have.get((w, piece), now + 1) <= now
                key = piece[0] * 4 + direct * also + spread * holders + noise * draw.random()
                if best is None or key < best[0]:
                    best = (key, piece)
            if best is not None:
                taken.add((v, best[1]))
                sends.append((u, v, best[1]))
        for u, v, piece in sends:
            have[v, piece] = now + 1
        slots.append(sends)
    ready = [max(have[p, (layer, q)] for p in range(square) for q in range(parts)) for layer in range(layers)]
    return slots, ready


def pick_kernel(choices, count, place, *refs):
    sources, outs, sems = refs[:-count - 1], refs[-count - 1 : -1], refs[-1]

    def copy_for(p):
        copies = []
        for n, per_device in enumerate(choices):
            operand, index = per_device[p]
            source = sources[operand] if index is None else sources[operand].at[index]
            copies.append(pltpu.make_async_copy(source, outs[n], sems.at[n]))
        for copy in copies:
            copy.start()
        for copy in copies:
            copy.wait()

    for p in range(len(choices[0])):
        pl.when(place[1] == p)(functools.partial(copy_for, p))


def pick(place, operands, in_hbm, choices, shape):
    smem = pl.BlockSpec(memory_space=pltpu.SMEM)
    return pl.pallas_call(
        functools.partial(pick_kernel, choices, len(choices)),
        out_shape=[pltpu.VMEM(shape, jnp.bfloat16)] * len(choices),
        in_specs=[smem] + [pl.BlockSpec(memory_space=pl.ANY)] * len(operands),
        out_specs=[pl.BlockSpec(memory_space=pltpu.VMEM)] * len(choices),
        scratch_shapes=[pltpu.SemaphoreType.DMA((len(choices),))],
        cost_estimate=BRIEF,
        compiler_params=pltpu.CompilerParams(vmem_limit_bytes=SMALL_VMEM),
    )(place, *pinned(operands, in_hbm))


def load_kernel(source, out, sem):
    copy = pltpu.make_async_copy(source, out, sem)
    copy.start()
    copy.wait()


def load(x):
    return pl.pallas_call(
        load_kernel,
        out_shape=pltpu.VMEM(x.shape, x.dtype),
        in_specs=[pl.BlockSpec(memory_space=pl.ANY)],
        out_specs=pl.BlockSpec(memory_space=pltpu.VMEM),
        scratch_shapes=[pltpu.SemaphoreType.DMA],
        cost_estimate=BRIEF,
        compiler_params=pltpu.CompilerParams(vmem_limit_bytes=SMALL_VMEM),
    )(pltpu.with_memory_space_constraint(x, pltpu.HBM))


class WeightStream:
    def __init__(self, weights, place, square, parts):
        self.weights, self.place = weights, place
        self.sections, self.parts = weights.shape[0], parts
        self.each = weights.shape[1] // parts
        self.slots, self.ready = stream_order(STREAM_SEED, square * self.sections, parts, square)
        self.square = square
        self.arrays = {}
        self.where = {}
        self.flying = []
        self.loaded = False
        self.started = 0
        self.gathered = {}

    def source(self, p, piece):
        if piece is None:
            piece = (p * self.sections, 0)
        if (p, piece) in self.where:
            return self.where[p, piece], None
        return "own", (piece[0] % self.sections, pl.ds(piece[1] * self.each, self.each))

    def array(self, name):
        return self.weights if name == "own" else self.arrays[name]

    def advance(self, after=(), through=()):
        sends = self.slots[self.started] if self.started < len(self.slots) else []
        sides = {}
        for u, v, piece in sends:
            sides.setdefault(u ^ v, {})[u] = piece
        chosen = {side: [self.source(p, by.get(p)) for p in range(self.square)] for side, by in sorted(sides.items())}
        names = sorted({name for items in chosen.values() for name, _ in items}, key=str)
        keys = self.flying + [n for n in names if n != "own" and n not in self.flying]
        _, held = lax.optimization_barrier((list(after), [self.arrays[k] for k in keys]))
        for key, value in zip(keys, held):
            self.arrays[key] = value
        self.flying = []
        if not sends:
            return list(through)
        choices = [[(names.index(name), index) for name, index in items] for items in chosen.values()]
        shape = (self.each,) + self.weights.shape[2:]
        in_hbm = [n for n, name in enumerate(names) if name == "own" and not self.loaded]
        picked = pick(self.place, [self.array(n) for n in names], in_hbm, choices, shape)
        for side, array in zip(chosen, picked):
            key = ("got", self.started, side)
            self.arrays[key] = lax.ppermute(array, "pipe", [(p, p ^ side) for p in range(self.square)])
            self.flying.append(key)
        for u, v, piece in sends:
            self.where[v, piece] = ("got", self.started, u ^ v)
        self.started += 1
        return lax.optimization_barrier((list(through), picked))[0]

    def gather(self, layer):
        if layer in self.gathered:
            return self.gathered[layer]
        names, plan = [], []
        for q in range(self.parts):
            for p in range(self.square):
                name, index = self.source(p, (layer, q))
                if name not in names:
                    names.append(name)
                plan.append((names.index(name), q * self.each, self.each, index, (1, p)))
        in_hbm = [n for n, name in enumerate(names) if name == "own" and not self.loaded]
        arrays = [self.array(name) for name in names]
        self.gathered[layer] = gather_weights(self.place, arrays, in_hbm, plan, self.weights.shape[1:])
        return self.gathered[layer]


def gather_square(x):
    mine = lax.axis_index("pipe")
    got = [x] + [lax.ppermute(x, "pipe", [(p, p ^ side) for p in range(4)]) for side in (1, 2, 3)]
    got = jnp.stack(got)
    return jnp.concatenate([lax.dynamic_index_in_dim(got, p ^ mine, 0, keepdims=False) for p in range(4)])


def on_device(features, weights, bias, layout):
    row_devs = lax.axis_size("rows")
    my_row = lax.axis_index("rows")
    neurons = features.shape[1]
    blocks = neurons // BLOCK
    slot_count = blocks * K
    pairs = neurons // LANES
    is_line = row_devs == 4 * CORES and lax.axis_size("pipe") == 4

    z = my_row // CORES
    is_middle = (z > 0) & (z < row_devs // CORES - 1)
    place = jnp.stack([is_middle.astype(jnp.int32), lax.axis_index("pipe").astype(jnp.int32)])
    if is_line:
        stream = WeightStream(weights, place, 4, WEIGHT_PARTS)
        layout, bias = stream.advance(through=[layout, bias])

    mine = lax.dynamic_slice_in_dim(layout, my_row * slot_count, slot_count, axis=1)
    owners, local = mine // blocks, mine % blocks
    table = line_slots(row_devs) if is_line else np.tile(np.arange(row_devs, dtype=np.int32), (row_devs, 1))
    my_slots = lax.dynamic_index_in_dim(jnp.asarray(table), my_row, 0, keepdims=False)
    hit = owners[:, :, None] == jnp.arange(row_devs)[None, None, :]
    slots = jnp.sum(jnp.where(hit, my_slots[None, None, :], 0), axis=2)
    codes = (((slots << bits_for(pairs)) | (local // 2)) << 1) | (local % 2)

    if is_line:
        base = 2 ** (bits_for(4 * CORES * pairs * 2) // 2)
        sent = jnp.concatenate([bias, *(part.astype(jnp.bfloat16) for part in (codes // base, codes % base))], axis=1)
        got = gather_square(sent)
        high, low = (
            got[:, neurons + n * slot_count : neurons + (n + 1) * slot_count].astype(jnp.int32) for n in range(2)
        )
        all_codes, all_bias = high * base + low, got[:, :neurons]
    else:
        all_codes = lax.all_gather(codes, "pipe", axis=0, tiled=True)
        all_bias = lax.all_gather(bias, "pipe", axis=0, tiled=True)
    layers = weights.shape[0] * lax.axis_size("pipe")

    current = features
    if is_line:
        for layer in range(layers):
            step = 0

            def pause(arrived, through):
                nonlocal step
                step += 1
                if layer == 0 and step == 1:
                    stream.weights = load(after_all(weights, *arrived))
                    stream.loaded = True
                if step == 1:
                    through = stream.advance(arrived + ([all_codes, all_bias] if layer == 0 else []), through)
                elif layer in BUSY_LAYERS:
                    through = stream.advance(arrived, through)
                if step == 2 and stream.started >= stream.ready[layer]:
                    through, _ = lax.optimization_barrier((through, stream.gather(layer)))
                return through

            split = stream.started == len(stream.slots)
            acts = gather_line(current, pause, split)
            while stream.started < stream.ready[layer] + (layer == 0):
                stream.advance()
            current = apply_layer(
                all_codes[layer], place, acts, line_plan(split), stream.gather(layer), all_bias[layer][None]
            )
        return current

    all_weights = lax.all_gather(weights, "pipe", axis=0, tiled=True)
    for layer in range(layers):
        acts = [lax.all_gather(current, "rows", axis=0, tiled=False)]
        act_plan = [(0, 0, row_devs, None)]
        current = apply_layer(
            all_codes[layer], place, acts, act_plan, all_weights[layer], all_bias[layer][None]
        )
    return current


def solution(mesh):
    in_specs = (
        P("pipe", "rows"),
        P("pipe", "rows", None, None),
        P("pipe", "rows"),
        P("pipe", None),
    )
    out_specs = P("pipe", "rows")
    return jax.shard_map(
        on_device, mesh=mesh, in_specs=in_specs, out_specs=out_specs, check_vma=False
    )
```

```python
import functools
import random

import jax
import jax.numpy as jnp
import numpy as np
from jax import lax
from jax.experimental import pallas as pl
from jax.experimental.pallas import tpu as pltpu
from jax.sharding import PartitionSpec as P

BLOCK = 64
K = 4
LANES = 128
CORES = 2
WEIGHT_PARTS = 4
STREAM_SEED = 486
BUSY_LAYERS = (0, 1, 3, 4)
LAYER_VMEM = 10 * 2**20
SMALL_VMEM = 2 * 2**20
BRIEF = pl.CostEstimate(flops=0, transcendentals=0, bytes_accessed=0)

clamp_top = 32.0


def bits_for(count):
    return (count - 1).bit_length()


def start_if(copy, place, want):
    if want is None:
        copy.start()
    else:
        pl.when(place[want[0]] == want[1])(copy.start)


def layer_kernel(act_plan, unroll, codes, place, *refs):
    n_acts = 1 + max(p[0] for p in act_plan)
    acts = refs[:n_acts]
    weights, bias, out, held, masks, act_sem = refs[n_acts:]
    rows = out.shape[0]
    blocks = weights.shape[0]
    pair_bits = bits_for(held.shape[2] // LANES)

    def act_copy(operand, slot, slots):
        src = acts[operand] if slots == 1 else acts[operand].at[:]
        dst = held.at[slot] if slots == 1 else held.at[pl.ds(slot, slots)]
        return pltpu.make_async_copy(src, dst, act_sem.at[slot])

    for operand, slot, slots, want in act_plan:
        start_if(act_copy(operand, slot, slots), place, want)

    low = lax.broadcasted_iota(jnp.int32, (rows, LANES), 1) < BLOCK
    masks[0] = jnp.where(low, 1.0, 0.0).astype(jnp.bfloat16)
    masks[1] = jnp.where(low, 0.0, 1.0).astype(jnp.bfloat16)

    waited = set()
    for operand, slot, slots, _ in act_plan:
        if slot not in waited:
            waited.add(slot)
            act_copy(operand, slot, slots).wait()

    def products(block):
        parts = []
        for k in range(K):
            code = codes[block * K + k]
            pair = (code >> 1) & (2**pair_bits - 1)
            columns = pl.ds(pl.multiple_of(pair * LANES, LANES), LANES)
            parts.append(held[code >> (1 + pair_bits), :, columns] * masks[code & 1])
        left = jnp.concatenate(
            [
                jnp.concatenate([parts[0], parts[2]], axis=1),
                jnp.concatenate([parts[1], parts[3]], axis=1),
            ],
            axis=0,
        )
        w = weights[block]
        first, second = w[:, :LANES], w[:, LANES:]
        right = jnp.concatenate([first, first, second, second], axis=0)
        return jnp.dot(left, right, preferred_element_type=jnp.float32)

    def two_blocks(q, _):
        a, b = products(2 * q), products(2 * q + 1)
        even = a[:rows] + pltpu.roll(a[rows:], BLOCK, 1)
        odd = b[rows:] + pltpu.roll(b[:rows], BLOCK, 1)
        columns = pl.ds(pl.multiple_of(q * LANES, LANES), LANES)
        total = jnp.where(low, even, odd) + bias[:, columns].astype(jnp.float32)
        out[:, columns] = jnp.clip(total, 0.0, clamp_top).astype(jnp.bfloat16)
        return 0

    lax.fori_loop(0, blocks // 2, two_blocks, 0, unroll=min(unroll, blocks // 2))


def gather_weights_kernel(plan, place, *refs):
    sources, out, sem = refs[:-2], refs[-2], refs[-1]

    def copy(operand, first, count, index):
        source = sources[operand] if index is None else sources[operand].at[index]
        return pltpu.make_async_copy(source, out.at[pl.ds(first, count)], sem.at[first])

    for operand, first, count, index, want in plan:
        start_if(copy(operand, first, count, index), place, want)
    for first, (operand, count, index) in {p[1]: (p[0], p[2], p[3]) for p in plan}.items():
        copy(operand, first, count, index).wait()


def pinned(operands, in_hbm):
    return [pltpu.with_memory_space_constraint(x, pltpu.HBM) if n in in_hbm else x for n, x in enumerate(operands)]


def gather_weights(place, weights, in_hbm, plan, shape):
    smem = pl.BlockSpec(memory_space=pltpu.SMEM)
    return pl.pallas_call(
        functools.partial(gather_weights_kernel, plan),
        out_shape=pltpu.VMEM(shape, jnp.bfloat16),
        in_specs=[smem] + [pl.BlockSpec(memory_space=pl.ANY)] * len(weights),
        out_specs=pl.BlockSpec(memory_space=pltpu.VMEM),
        scratch_shapes=[pltpu.SemaphoreType.DMA((shape[0],))],
        cost_estimate=BRIEF,
        compiler_params=pltpu.CompilerParams(vmem_limit_bytes=SMALL_VMEM),
    )(place, *pinned(weights, in_hbm))


def apply_layer(codes, place, acts, act_plan, weights, bias):
    slots = sum(
        count for slot, count in {(slot, count) for _, slot, count, _ in act_plan}
    )
    rows, neurons = acts[0].shape[-2:]
    held = (slots, rows, neurons)
    smem = pl.BlockSpec(memory_space=pltpu.SMEM)
    anywhere = pl.BlockSpec(memory_space=pl.ANY)
    vmem = pl.BlockSpec(memory_space=pltpu.VMEM)
    kernel = functools.partial(layer_kernel, act_plan, 16)
    return pl.pallas_call(
        kernel,
        out_shape=jax.ShapeDtypeStruct((rows, neurons), jnp.bfloat16),
        in_specs=[smem, smem] + [anywhere] * len(acts) + [vmem, vmem],
        out_specs=vmem,
        scratch_shapes=[
            pltpu.VMEM(held, jnp.bfloat16),
            pltpu.VMEM((2, rows, LANES), jnp.bfloat16),
            pltpu.SemaphoreType.DMA((slots,)),
        ],
        cost_estimate=BRIEF,
        compiler_params=pltpu.CompilerParams(vmem_limit_bytes=LAYER_VMEM),
    )(codes, place, *acts, weights, bias)


def along_line(x, pairs):
    moves = [(a * CORES + c, b * CORES + c) for a, b in pairs for c in range(CORES)]
    return lax.ppermute(x, "rows", moves)


def to_other_core(x):
    return lax.ppermute(x, "rows", [(i, i ^ 1) for i in range(lax.axis_size("rows"))])


def after_all(x, *arrived):
    return lax.optimization_barrier((x, *arrived))[0]


def gather_line(x, pause, split):
    inside, ends = [(1, 2), (2, 1)], [(0, 3), (3, 0)]
    near = along_line(x, [(0, 1), (1, 0), (2, 3), (3, 2)])
    cross = along_line(x, inside if split else inside + ends)
    trade = [along_line(x, ends)] if split else []
    x_swapped = to_other_core(x)
    near, cross = pause([x_swapped], [near, cross])
    far = along_line(near, inside)
    outer = along_line(cross, [(2, 3), (1, 0)])
    near_swapped, cross_swapped = to_other_core(near), to_other_core(cross)
    (outer,) = pause([near_swapped], [outer])
    rest = [far, outer] + trade
    swapped = [x_swapped, near_swapped, cross_swapped] + [to_other_core(buf) for buf in rest]
    return [x, near, cross] + rest + swapped


def line_plan(split):
    middle, ends = (0, 1), (0, 0)
    where = [(0, None), (1, None), (2, middle if split else None), (3, middle), (3, ends), (2, ends)]
    where = where[: 6 if split else 5]
    return [
        (side * len(where) + buf, side * 4 + slot, 1, want)
        for side in range(CORES)
        for buf, (slot, want) in enumerate(where)
    ]


def line_slots(row_devs):
    table = np.zeros((row_devs, row_devs), np.int32)
    chips = row_devs // CORES
    for me in range(row_devs):
        for owner in range(row_devs):
            z, c = divmod(me, CORES)
            oz, oc = divmod(owner, CORES)
            if oz // 2 == z // 2:
                slot = 0 if oz == z else 1
            else:
                across = chips - 1 - z
                slot = 2 if oz == across else 3
            table[me, owner] = (c != oc) * chips + slot
    return table


def stream_order(seed, layers, parts, square):
    draw = random.Random(seed)
    each = layers // square
    links = [(u, u ^ 1) for u in range(square)] + [(u, u ^ 2) for u in range(square)]
    pieces = [(layer, q) for layer in range(layers) for q in range(parts)]
    have = {(p, piece): 0 for p in range(square) for piece in pieces if piece[0] // each == p}
    noise, direct, spread = draw.choice([0, 0.3, 1, 2]), draw.choice([0, 1, 2]), draw.choice([0, 0.5, 1, 2])
    slots = []
    while len(have) < square * len(pieces):
        now, sends = len(slots), []
        taken = set()
        order = links[:]
        draw.shuffle(order)
        if now == 0:
            sends = [(u, v, (u * each, 0 if u ^ v == 1 else 1)) for u, v in links]
            order = []
        for u, v in order:
            best = None
            for piece in pieces:
                if (v, piece) in have or (v, piece) in taken or have.get((u, piece), now + 1) > now:
                    continue
                w = v ^ 1 if u == v ^ 2 else v ^ 2
                holders = sum((p, piece) in have or (p, piece) in taken for p in range(square))
                also = have.get((w, piece), now + 1) <= now
                key = piece[0] * 4 + direct * also + spread * holders + noise * draw.random()
                if best is None or key < best[0]:
                    best = (key, piece)
            if best is not None:
                taken.add((v, best[1]))
                sends.append((u, v, best[1]))
        for u, v, piece in sends:
            have[v, piece] = now + 1
        slots.append(sends)
    ready = [max(have[p, (layer, q)] for p in range(square) for q in range(parts)) for layer in range(layers)]
    return slots, ready


def pick_kernel(choices, count, place, *refs):
    sources, outs, sems = refs[:-count - 1], refs[-count - 1 : -1], refs[-1]

    def copy_for(p):
        copies = []
        for n, per_device in enumerate(choices):
            operand, index = per_device[p]
            source = sources[operand] if index is None else sources[operand].at[index]
            copies.append(pltpu.make_async_copy(source, outs[n], sems.at[n]))
        for copy in copies:
            copy.start()
        for copy in copies:
            copy.wait()

    for p in range(len(choices[0])):
        pl.when(place[1] == p)(functools.partial(copy_for, p))


def pick(place, operands, in_hbm, choices, shape):
    smem = pl.BlockSpec(memory_space=pltpu.SMEM)
    return pl.pallas_call(
        functools.partial(pick_kernel, choices, len(choices)),
        out_shape=[pltpu.VMEM(shape, jnp.bfloat16)] * len(choices),
        in_specs=[smem] + [pl.BlockSpec(memory_space=pl.ANY)] * len(operands),
        out_specs=[pl.BlockSpec(memory_space=pltpu.VMEM)] * len(choices),
        scratch_shapes=[pltpu.SemaphoreType.DMA((len(choices),))],
        cost_estimate=BRIEF,
        compiler_params=pltpu.CompilerParams(vmem_limit_bytes=SMALL_VMEM),
    )(place, *pinned(operands, in_hbm))


def load_kernel(source, out, sem):
    copy = pltpu.make_async_copy(source, out, sem)
    copy.start()
    copy.wait()


def load(x):
    return pl.pallas_call(
        load_kernel,
        out_shape=pltpu.VMEM(x.shape, x.dtype),
        in_specs=[pl.BlockSpec(memory_space=pl.ANY)],
        out_specs=pl.BlockSpec(memory_space=pltpu.VMEM),
        scratch_shapes=[pltpu.SemaphoreType.DMA],
        cost_estimate=BRIEF,
        compiler_params=pltpu.CompilerParams(vmem_limit_bytes=SMALL_VMEM),
    )(pltpu.with_memory_space_constraint(x, pltpu.HBM))


class WeightStream:
    def __init__(self, weights, place, square, parts):
        self.weights, self.place = weights, place
        self.sections, self.parts = weights.shape[0], parts
        self.each = weights.shape[1] // parts
        self.slots, self.ready = stream_order(STREAM_SEED, square * self.sections, parts, square)
        self.square = square
        self.arrays = {}
        self.where = {}
        self.flying = []
        self.loaded = False
        self.started = 0
        self.gathered = {}

    def source(self, p, piece):
        if piece is None:
            piece = (p * self.sections, 0)
        if (p, piece) in self.where:
            return self.where[p, piece], None
        return "own", (piece[0] % self.sections, pl.ds(piece[1] * self.each, self.each))

    def array(self, name):
        return self.weights if name == "own" else self.arrays[name]

    def advance(self, after=(), through=()):
        sends = self.slots[self.started] if self.started < len(self.slots) else []
        sides = {}
        for u, v, piece in sends:
            sides.setdefault(u ^ v, {})[u] = piece
        chosen = {side: [self.source(p, by.get(p)) for p in range(self.square)] for side, by in sorted(sides.items())}
        names = sorted({name for items in chosen.values() for name, _ in items}, key=str)
        keys = self.flying + [n for n in names if n != "own" and n not in self.flying]
        _, held = lax.optimization_barrier((list(after), [self.arrays[k] for k in keys]))
        for key, value in zip(keys, held):
            self.arrays[key] = value
        self.flying = []
        if not sends:
            return list(through)
        choices = [[(names.index(name), index) for name, index in items] for items in chosen.values()]
        shape = (self.each,) + self.weights.shape[2:]
        in_hbm = [n for n, name in enumerate(names) if name == "own" and not self.loaded]
        picked = pick(self.place, [self.array(n) for n in names], in_hbm, choices, shape)
        for side, array in zip(chosen, picked):
            key = ("got", self.started, side)
            self.arrays[key] = lax.ppermute(array, "pipe", [(p, p ^ side) for p in range(self.square)])
            self.flying.append(key)
        for u, v, piece in sends:
            self.where[v, piece] = ("got", self.started, u ^ v)
        self.started += 1
        return lax.optimization_barrier((list(through), picked))[0]

    def gather(self, layer):
        if layer in self.gathered:
            return self.gathered[layer]
        names, plan = [], []
        for q in range(self.parts):
            for p in range(self.square):
                name, index = self.source(p, (layer, q))
                if name not in names:
                    names.append(name)
                plan.append((names.index(name), q * self.each, self.each, index, (1, p)))
        in_hbm = [n for n, name in enumerate(names) if name == "own" and not self.loaded]
        arrays = [self.array(name) for name in names]
        self.gathered[layer] = gather_weights(self.place, arrays, in_hbm, plan, self.weights.shape[1:])
        return self.gathered[layer]


def gather_square(x):
    mine = lax.axis_index("pipe")
    got = [x] + [lax.ppermute(x, "pipe", [(p, p ^ side) for p in range(4)]) for side in (1, 2, 3)]
    got = jnp.stack(got)
    return jnp.concatenate([lax.dynamic_index_in_dim(got, p ^ mine, 0, keepdims=False) for p in range(4)])


def on_device(features, weights, bias, layout):
    row_devs = lax.axis_size("rows")
    my_row = lax.axis_index("rows")
    neurons = features.shape[1]
    blocks = neurons // BLOCK
    slot_count = blocks * K
    pairs = neurons // LANES
    is_line = row_devs == 4 * CORES and lax.axis_size("pipe") == 4

    z = my_row // CORES
    is_middle = (z > 0) & (z < row_devs // CORES - 1)
    place = jnp.stack([is_middle.astype(jnp.int32), lax.axis_index("pipe").astype(jnp.int32)])
    if is_line:
        stream = WeightStream(weights, place, 4, WEIGHT_PARTS)
        layout, bias = stream.advance(through=[layout, bias])

    mine = lax.dynamic_slice_in_dim(layout, my_row * slot_count, slot_count, axis=1)
    owners, local = mine // blocks, mine % blocks
    table = line_slots(row_devs) if is_line else np.tile(np.arange(row_devs, dtype=np.int32), (row_devs, 1))
    my_slots = lax.dynamic_index_in_dim(jnp.asarray(table), my_row, 0, keepdims=False)
    hit = owners[:, :, None] == jnp.arange(row_devs)[None, None, :]
    slots = jnp.sum(jnp.where(hit, my_slots[None, None, :], 0), axis=2)
    codes = (((slots << bits_for(pairs)) | (local // 2)) << 1) | (local % 2)

    if is_line:
        base = 2 ** (bits_for(4 * CORES * pairs * 2) // 2)
        sent = jnp.concatenate([bias, *(part.astype(jnp.bfloat16) for part in (codes // base, codes % base))], axis=1)
        got = gather_square(sent)
        high, low = (
            got[:, neurons + n * slot_count : neurons + (n + 1) * slot_count].astype(jnp.int32) for n in range(2)
        )
        all_codes, all_bias = high * base + low, got[:, :neurons]
    else:
        all_codes = lax.all_gather(codes, "pipe", axis=0, tiled=True)
        all_bias = lax.all_gather(bias, "pipe", axis=0, tiled=True)
    layers = weights.shape[0] * lax.axis_size("pipe")

    current = features
    if is_line:
        for layer in range(layers):
            step = 0

            def pause(arrived, through):
                nonlocal step
                step += 1
                if layer == 0 and step == 1:
                    stream.weights = load(after_all(weights, *arrived))
                    stream.loaded = True
                if step == 1:
                    through = stream.advance(arrived + ([all_codes, all_bias] if layer == 0 else []), through)
                elif layer in BUSY_LAYERS:
                    through = stream.advance(arrived, through)
                if step == 2 and stream.started >= stream.ready[layer]:
                    through, _ = lax.optimization_barrier((through, stream.gather(layer)))
                return through

            split = stream.started == len(stream.slots)
            acts = gather_line(current, pause, split)
            while stream.started < stream.ready[layer] + (layer == 0):
                stream.advance()
            current = apply_layer(
                all_codes[layer], place, acts, line_plan(split), stream.gather(layer), all_bias[layer][None]
            )
        return current

    all_weights = lax.all_gather(weights, "pipe", axis=0, tiled=True)
    for layer in range(layers):
        acts = [lax.all_gather(current, "rows", axis=0, tiled=False)]
        act_plan = [(0, 0, row_devs, None)]
        current = apply_layer(
            all_codes[layer], place, acts, act_plan, all_weights[layer], all_bias[layer][None]
        )
    return current


def solution(mesh):
    in_specs = (
        P("pipe", "rows"),
        P("pipe", "rows", None, None),
        P("pipe", "rows"),
        P("pipe", None),
    )
    out_specs = P("pipe", "rows")
    return jax.shard_map(
        on_device, mesh=mesh, in_specs=in_specs, out_specs=out_specs, check_vma=False
    )
```

```python
import functools
import random

import jax
import jax.numpy as jnp
import numpy as np
from jax import lax
from jax.experimental import pallas as pl
from jax.experimental.pallas import tpu as pltpu
from jax.sharding import PartitionSpec as P

BLOCK = 64
K = 4
LANES = 128
CORES = 2
WEIGHT_PARTS = 4
STREAM_SEED = 486
BUSY_LAYERS = (0, 1, 3, 4)
LAYER_VMEM = 10 * 2**20
SMALL_VMEM = 2 * 2**20
BRIEF = pl.CostEstimate(flops=0, transcendentals=0, bytes_accessed=0)

clamp_top = 32.0


def bits_for(count):
    return (count - 1).bit_length()


def start_if(copy, place, want):
    if want is None:
        copy.start()
    else:
        pl.when(place[want[0]] == want[1])(copy.start)


def layer_kernel(act_plan, unroll, codes, place, *refs):
    n_acts = 1 + max(p[0] for p in act_plan)
    acts = refs[:n_acts]
    weights, bias, out, held, masks, act_sem = refs[n_acts:]
    rows = out.shape[0]
    blocks = weights.shape[0]
    pair_bits = bits_for(held.shape[2] // LANES)

    def act_copy(operand, slot, slots):
        src = acts[operand] if slots == 1 else acts[operand].at[:]
        dst = held.at[slot] if slots == 1 else held.at[pl.ds(slot, slots)]
        return pltpu.make_async_copy(src, dst, act_sem.at[slot])

    for operand, slot, slots, want in act_plan:
        start_if(act_copy(operand, slot, slots), place, want)

    low = lax.broadcasted_iota(jnp.int32, (rows, LANES), 1) < BLOCK
    masks[0] = jnp.where(low, 1.0, 0.0).astype(jnp.bfloat16)
    masks[1] = jnp.where(low, 0.0, 1.0).astype(jnp.bfloat16)

    waited = set()
    for operand, slot, slots, _ in act_plan:
        if slot not in waited:
            waited.add(slot)
            act_copy(operand, slot, slots).wait()

    def products(block):
        parts = []
        for k in range(K):
            code = codes[block * K + k]
            pair = (code >> 1) & (2**pair_bits - 1)
            columns = pl.ds(pl.multiple_of(pair * LANES, LANES), LANES)
            parts.append(held[code >> (1 + pair_bits), :, columns] * masks[code & 1])
        left = jnp.concatenate(
            [
                jnp.concatenate([parts[0], parts[2]], axis=1),
                jnp.concatenate([parts[1], parts[3]], axis=1),
            ],
            axis=0,
        )
        w = weights[block]
        first, second = w[:, :LANES], w[:, LANES:]
        right = jnp.concatenate([first, first, second, second], axis=0)
        return jnp.dot(left, right, preferred_element_type=jnp.float32)

    def two_blocks(q, _):
        a, b = products(2 * q), products(2 * q + 1)
        even = a[:rows] + pltpu.roll(a[rows:], BLOCK, 1)
        odd = b[rows:] + pltpu.roll(b[:rows], BLOCK, 1)
        columns = pl.ds(pl.multiple_of(q * LANES, LANES), LANES)
        total = jnp.where(low, even, odd) + bias[:, columns].astype(jnp.float32)
        out[:, columns] = jnp.clip(total, 0.0, clamp_top).astype(jnp.bfloat16)
        return 0

    lax.fori_loop(0, blocks // 2, two_blocks, 0, unroll=min(unroll, blocks // 2))


def gather_weights_kernel(plan, place, *refs):
    sources, out, sem = refs[:-2], refs[-2], refs[-1]

    def copy(operand, first, count, index):
        source = sources[operand] if index is None else sources[operand].at[index]
        return pltpu.make_async_copy(source, out.at[pl.ds(first, count)], sem.at[first])

    for operand, first, count, index, want in plan:
        start_if(copy(operand, first, count, index), place, want)
    for first, (operand, count, index) in {p[1]: (p[0], p[2], p[3]) for p in plan}.items():
        copy(operand, first, count, index).wait()


def pinned(operands, in_hbm):
    return [pltpu.with_memory_space_constraint(x, pltpu.HBM) if n in in_hbm else x for n, x in enumerate(operands)]


def gather_weights(place, weights, in_hbm, plan, shape):
    smem = pl.BlockSpec(memory_space=pltpu.SMEM)
    return pl.pallas_call(
        functools.partial(gather_weights_kernel, plan),
        out_shape=pltpu.VMEM(shape, jnp.bfloat16),
        in_specs=[smem] + [pl.BlockSpec(memory_space=pl.ANY)] * len(weights),
        out_specs=pl.BlockSpec(memory_space=pltpu.VMEM),
        scratch_shapes=[pltpu.SemaphoreType.DMA((shape[0],))],
        cost_estimate=BRIEF,
        compiler_params=pltpu.CompilerParams(vmem_limit_bytes=SMALL_VMEM),
    )(place, *pinned(weights, in_hbm))


def apply_layer(codes, place, acts, act_plan, weights, bias):
    slots = sum(
        count for slot, count in {(slot, count) for _, slot, count, _ in act_plan}
    )
    rows, neurons = acts[0].shape[-2:]
    held = (slots, rows, neurons)
    smem = pl.BlockSpec(memory_space=pltpu.SMEM)
    anywhere = pl.BlockSpec(memory_space=pl.ANY)
    vmem = pl.BlockSpec(memory_space=pltpu.VMEM)
    kernel = functools.partial(layer_kernel, act_plan, 32)
    return pl.pallas_call(
        kernel,
        out_shape=jax.ShapeDtypeStruct((rows, neurons), jnp.bfloat16),
        in_specs=[smem, smem] + [anywhere] * len(acts) + [vmem, vmem],
        out_specs=vmem,
        scratch_shapes=[
            pltpu.VMEM(held, jnp.bfloat16),
            pltpu.VMEM((2, rows, LANES), jnp.bfloat16),
            pltpu.SemaphoreType.DMA((slots,)),
        ],
        cost_estimate=BRIEF,
        compiler_params=pltpu.CompilerParams(vmem_limit_bytes=LAYER_VMEM),
    )(codes, place, *acts, weights, bias)


def along_line(x, pairs):
    moves = [(a * CORES + c, b * CORES + c) for a, b in pairs for c in range(CORES)]
    return lax.ppermute(x, "rows", moves)


def to_other_core(x):
    return lax.ppermute(x, "rows", [(i, i ^ 1) for i in range(lax.axis_size("rows"))])


def after_all(x, *arrived):
    return lax.optimization_barrier((x, *arrived))[0]


def gather_line(x, pause, split):
    inside, ends = [(1, 2), (2, 1)], [(0, 3), (3, 0)]
    near = along_line(x, [(0, 1), (1, 0), (2, 3), (3, 2)])
    cross = along_line(x, inside if split else inside + ends)
    trade = [along_line(x, ends)] if split else []
    x_swapped = to_other_core(x)
    near, cross = pause([x_swapped], [near, cross])
    far = along_line(near, inside)
    outer = along_line(cross, [(2, 3), (1, 0)])
    near_swapped, cross_swapped = to_other_core(near), to_other_core(cross)
    (outer,) = pause([near_swapped], [outer])
    rest = [far, outer] + trade
    swapped = [x_swapped, near_swapped, cross_swapped] + [to_other_core(buf) for buf in rest]
    return [x, near, cross] + rest + swapped


def line_plan(split):
    middle, ends = (0, 1), (0, 0)
    where = [(0, None), (1, None), (2, middle if split else None), (3, middle), (3, ends), (2, ends)]
    where = where[: 6 if split else 5]
    return [
        (side * len(where) + buf, side * 4 + slot, 1, want)
        for side in range(CORES)
        for buf, (slot, want) in enumerate(where)
    ]


def line_slots(row_devs):
    table = np.zeros((row_devs, row_devs), np.int32)
    chips = row_devs // CORES
    for me in range(row_devs):
        for owner in range(row_devs):
            z, c = divmod(me, CORES)
            oz, oc = divmod(owner, CORES)
            if oz // 2 == z // 2:
                slot = 0 if oz == z else 1
            else:
                across = chips - 1 - z
                slot = 2 if oz == across else 3
            table[me, owner] = (c != oc) * chips + slot
    return table


def stream_order(seed, layers, parts, square):
    draw = random.Random(seed)
    each = layers // square
    links = [(u, u ^ 1) for u in range(square)] + [(u, u ^ 2) for u in range(square)]
    pieces = [(layer, q) for layer in range(layers) for q in range(parts)]
    have = {(p, piece): 0 for p in range(square) for piece in pieces if piece[0] // each == p}
    noise, direct, spread = draw.choice([0, 0.3, 1, 2]), draw.choice([0, 1, 2]), draw.choice([0, 0.5, 1, 2])
    slots = []
    while len(have) < square * len(pieces):
        now, sends = len(slots), []
        taken = set()
        order = links[:]
        draw.shuffle(order)
        if now == 0:
            sends = [(u, v, (u * each, 0 if u ^ v == 1 else 1)) for u, v in links]
            order = []
        for u, v in order:
            best = None
            for piece in pieces:
                if (v, piece) in have or (v, piece) in taken or have.get((u, piece), now + 1) > now:
                    continue
                w = v ^ 1 if u == v ^ 2 else v ^ 2
                holders = sum((p, piece) in have or (p, piece) in taken for p in range(square))
                also = have.get((w, piece), now + 1) <= now
                key = piece[0] * 4 + direct * also + spread * holders + noise * draw.random()
                if best is None or key < best[0]:
                    best = (key, piece)
            if best is not None:
                taken.add((v, best[1]))
                sends.append((u, v, best[1]))
        for u, v, piece in sends:
            have[v, piece] = now + 1
        slots.append(sends)
    ready = [max(have[p, (layer, q)] for p in range(square) for q in range(parts)) for layer in range(layers)]
    return slots, ready


def pick_kernel(choices, count, place, *refs):
    sources, outs, sems = refs[:-count - 1], refs[-count - 1 : -1], refs[-1]

    def copy_for(p):
        copies = []
        for n, per_device in enumerate(choices):
            operand, index = per_device[p]
            source = sources[operand] if index is None else sources[operand].at[index]
            copies.append(pltpu.make_async_copy(source, outs[n], sems.at[n]))
        for copy in copies:
            copy.start()
        for copy in copies:
            copy.wait()

    for p in range(len(choices[0])):
        pl.when(place[1] == p)(functools.partial(copy_for, p))


def pick(place, operands, in_hbm, choices, shape):
    smem = pl.BlockSpec(memory_space=pltpu.SMEM)
    return pl.pallas_call(
        functools.partial(pick_kernel, choices, len(choices)),
        out_shape=[pltpu.VMEM(shape, jnp.bfloat16)] * len(choices),
        in_specs=[smem] + [pl.BlockSpec(memory_space=pl.ANY)] * len(operands),
        out_specs=[pl.BlockSpec(memory_space=pltpu.VMEM)] * len(choices),
        scratch_shapes=[pltpu.SemaphoreType.DMA((len(choices),))],
        cost_estimate=BRIEF,
        compiler_params=pltpu.CompilerParams(vmem_limit_bytes=SMALL_VMEM),
    )(place, *pinned(operands, in_hbm))


def load_kernel(source, out, sem):
    copy = pltpu.make_async_copy(source, out, sem)
    copy.start()
    copy.wait()


def load(x):
    return pl.pallas_call(
        load_kernel,
        out_shape=pltpu.VMEM(x.shape, x.dtype),
        in_specs=[pl.BlockSpec(memory_space=pl.ANY)],
        out_specs=pl.BlockSpec(memory_space=pltpu.VMEM),
        scratch_shapes=[pltpu.SemaphoreType.DMA],
        cost_estimate=BRIEF,
        compiler_params=pltpu.CompilerParams(vmem_limit_bytes=SMALL_VMEM),
    )(pltpu.with_memory_space_constraint(x, pltpu.HBM))


class WeightStream:
    def __init__(self, weights, place, square, parts):
        self.weights, self.place = weights, place
        self.sections, self.parts = weights.shape[0], parts
        self.each = weights.shape[1] // parts
        self.slots, self.ready = stream_order(STREAM_SEED, square * self.sections, parts, square)
        self.square = square
        self.arrays = {}
        self.where = {}
        self.flying = []
        self.loaded = False
        self.started = 0
        self.gathered = {}

    def source(self, p, piece):
        if piece is None:
            piece = (p * self.sections, 0)
        if (p, piece) in self.where:
            return self.where[p, piece], None
        return "own", (piece[0] % self.sections, pl.ds(piece[1] * self.each, self.each))

    def array(self, name):
        return self.weights if name == "own" else self.arrays[name]

    def advance(self, after=(), through=()):
        sends = self.slots[self.started] if self.started < len(self.slots) else []
        sides = {}
        for u, v, piece in sends:
            sides.setdefault(u ^ v, {})[u] = piece
        chosen = {side: [self.source(p, by.get(p)) for p in range(self.square)] for side, by in sorted(sides.items())}
        names = sorted({name for items in chosen.values() for name, _ in items}, key=str)
        keys = self.flying + [n for n in names if n != "own" and n not in self.flying]
        _, held = lax.optimization_barrier((list(after), [self.arrays[k] for k in keys]))
        for key, value in zip(keys, held):
            self.arrays[key] = value
        self.flying = []
        if not sends:
            return list(through)
        choices = [[(names.index(name), index) for name, index in items] for items in chosen.values()]
        shape = (self.each,) + self.weights.shape[2:]
        in_hbm = [n for n, name in enumerate(names) if name == "own" and not self.loaded]
        picked = pick(self.place, [self.array(n) for n in names], in_hbm, choices, shape)
        for side, array in zip(chosen, picked):
            key = ("got", self.started, side)
            self.arrays[key] = lax.ppermute(array, "pipe", [(p, p ^ side) for p in range(self.square)])
            self.flying.append(key)
        for u, v, piece in sends:
            self.where[v, piece] = ("got", self.started, u ^ v)
        self.started += 1
        return lax.optimization_barrier((list(through), picked))[0]

    def gather(self, layer):
        if layer in self.gathered:
            return self.gathered[layer]
        names, plan = [], []
        for q in range(self.parts):
            for p in range(self.square):
                name, index = self.source(p, (layer, q))
                if name not in names:
                    names.append(name)
                plan.append((names.index(name), q * self.each, self.each, index, (1, p)))
        in_hbm = [n for n, name in enumerate(names) if name == "own" and not self.loaded]
        arrays = [self.array(name) for name in names]
        self.gathered[layer] = gather_weights(self.place, arrays, in_hbm, plan, self.weights.shape[1:])
        return self.gathered[layer]


def gather_square(x):
    mine = lax.axis_index("pipe")
    got = [x] + [lax.ppermute(x, "pipe", [(p, p ^ side) for p in range(4)]) for side in (1, 2, 3)]
    got = jnp.stack(got)
    return jnp.concatenate([lax.dynamic_index_in_dim(got, p ^ mine, 0, keepdims=False) for p in range(4)])


def on_device(features, weights, bias, layout):
    row_devs = lax.axis_size("rows")
    my_row = lax.axis_index("rows")
    neurons = features.shape[1]
    blocks = neurons // BLOCK
    slot_count = blocks * K
    pairs = neurons // LANES
    is_line = row_devs == 4 * CORES and lax.axis_size("pipe") == 4

    z = my_row // CORES
    is_middle = (z > 0) & (z < row_devs // CORES - 1)
    place = jnp.stack([is_middle.astype(jnp.int32), lax.axis_index("pipe").astype(jnp.int32)])
    if is_line:
        stream = WeightStream(weights, place, 4, WEIGHT_PARTS)
        layout, bias = stream.advance(through=[layout, bias])

    mine = lax.dynamic_slice_in_dim(layout, my_row * slot_count, slot_count, axis=1)
    owners, local = mine // blocks, mine % blocks
    table = line_slots(row_devs) if is_line else np.tile(np.arange(row_devs, dtype=np.int32), (row_devs, 1))
    my_slots = lax.dynamic_index_in_dim(jnp.asarray(table), my_row, 0, keepdims=False)
    hit = owners[:, :, None] == jnp.arange(row_devs)[None, None, :]
    slots = jnp.sum(jnp.where(hit, my_slots[None, None, :], 0), axis=2)
    codes = (((slots << bits_for(pairs)) | (local // 2)) << 1) | (local % 2)

    if is_line:
        base = 2 ** (bits_for(4 * CORES * pairs * 2) // 2)
        sent = jnp.concatenate([bias, *(part.astype(jnp.bfloat16) for part in (codes // base, codes % base))], axis=1)
        got = gather_square(sent)
        high, low = (
            got[:, neurons + n * slot_count : neurons + (n + 1) * slot_count].astype(jnp.int32) for n in range(2)
        )
        all_codes, all_bias = high * base + low, got[:, :neurons]
    else:
        all_codes = lax.all_gather(codes, "pipe", axis=0, tiled=True)
        all_bias = lax.all_gather(bias, "pipe", axis=0, tiled=True)
    layers = weights.shape[0] * lax.axis_size("pipe")

    current = features
    if is_line:
        for layer in range(layers):
            step = 0

            def pause(arrived, through):
                nonlocal step
                step += 1
                if layer == 0 and step == 1:
                    stream.weights = load(after_all(weights, *arrived))
                    stream.loaded = True
                if step == 1:
                    through = stream.advance(arrived + ([all_codes, all_bias] if layer == 0 else []), through)
                elif layer in BUSY_LAYERS:
                    through = stream.advance(arrived, through)
                if step == 2 and stream.started >= stream.ready[layer]:
                    through, _ = lax.optimization_barrier((through, stream.gather(layer)))
                return through

            split = stream.started == len(stream.slots)
            acts = gather_line(current, pause, split)
            while stream.started < stream.ready[layer] + (layer == 0):
                stream.advance()
            current = apply_layer(
                all_codes[layer], place, acts, line_plan(split), stream.gather(layer), all_bias[layer][None]
            )
        return current

    all_weights = lax.all_gather(weights, "pipe", axis=0, tiled=True)
    for layer in range(layers):
        acts = [lax.all_gather(current, "rows", axis=0, tiled=False)]
        act_plan = [(0, 0, row_devs, None)]
        current = apply_layer(
            all_codes[layer], place, acts, act_plan, all_weights[layer], all_bias[layer][None]
        )
    return current


def solution(mesh):
    in_specs = (
        P("pipe", "rows"),
        P("pipe", "rows", None, None),
        P("pipe", "rows"),
        P("pipe", None),
    )
    out_specs = P("pipe", "rows")
    return jax.shard_map(
        on_device, mesh=mesh, in_specs=in_specs, out_specs=out_specs, check_vma=False
    )
```
